512 devices in a mesh: vocab: 64 (over x, z), rows: 8 (over y, core).
Axes of the slice: x: 4, y: 4, z: 16, core: 2. Of those that a mesh axis runs over, the one named last changes fastest.
Arguments:
- hidden: bfloat16 [384, 8192], P('vocab', 'rows'), may hold values from -24 to 24
- head: bfloat16 [76032, 8192], P('vocab', 'rows'), may hold values from -0.2 to 0.2
- targets: int32 [384], replicated, may hold values from 0 to 76031
- upstream: float32 [384], replicated, may hold values from 4 to 40
Outputs:
- token_loss: float32 [384], P('rows')
- grad_hidden: bfloat16 [384, 8192], P('vocab', 'rows')
- grad_head: bfloat16 [76032, 8192], P('vocab', 'rows')
The draws below stay inside these ranges and needn't reach their ends.
All inputs are finite; a program needn't handle non-finite values.
Results may differ from the reference program's by a relative error of at most 0.006.
Values may be sent and summed in bfloat16 or wider, within the bound.
No kernel may reach another device: no remote copies, remote signals or barrier semaphores. Data moves between devices by JAX's collectives and lax.ppermute only.
A program may use at most 64 MiB of HBM per device.

```python
import math
import jax
import jax.numpy as jnp
from jax import lax

D = 8192
V_DEV = 1188
VOCAB = 76032
TOKENS = 384
N_VOCAB = 64


def base_head(key):
    values = jax.random.normal(key, (VOCAB, D), jnp.float32) * (3.0 / D ** 0.5)
    return jnp.clip(values, -0.19, 0.19)


def draw_head(key, part):
    values = base_head(key)
    return values.astype(jnp.bfloat16)


def draw_hidden(key, part):
    key = jax.random.fold_in(key, 23)
    values = jnp.clip(jax.random.normal(key, (TOKENS, D), jnp.float32), -6.0, 6.0)
    return values.astype(jnp.bfloat16)


def place_ends(drawn, key, low, high):
    longest = drawn.shape.index(max(drawn.shape))
    spots = []
    for shift in (0, 1):
        where = [jax.random.randint(jax.random.fold_in(key, axis), (), 0, length) for axis, length in enumerate(drawn.shape)]
        where[longest] = (where[longest] + shift) % drawn.shape[longest]
        spots.append(tuple(where))
    return drawn.at[spots[0]].set(low).at[spots[1]].set(high)


def setup_inputs(seed: int = 0) -> dict:
    keys = jax.random.split(jax.random.key(seed), 5)
    return {
        "hidden": draw_hidden(jax.random.fold_in(keys[4], 71), 0),
        "head": draw_head(jax.random.fold_in(keys[4], 71), 0),
        "targets": place_ends(jax.random.randint(keys[2], (TOKENS,), 0, VOCAB), jax.random.fold_in(keys[2], 1), 0, VOCAB - 1).astype(jnp.int32),
        "upstream": jnp.clip(jnp.exp(jax.random.uniform(keys[3], (TOKENS,), jnp.float32, math.log(4.0), math.log(40.0))), 4.0, 40.0),
    }


def reference(hidden, head, targets, upstream):
    logits = lax.dot_general(hidden, head, (((1,), (1,)), ((), ())), preferred_element_type=jnp.float32)
    row_top = jnp.max(logits, axis=1)
    lse = row_top + jnp.log(jnp.sum(jnp.exp(logits - row_top[:, None]), axis=1))
    columns = lax.broadcasted_iota(jnp.int32, logits.shape, 1)
    target_mask = columns == targets[:, None]
    target_logit = jnp.sum(jnp.where(target_mask, logits, jnp.float32(0.0)), axis=1)
    token_loss = lse - target_logit
    probability = jnp.exp(logits - lse[:, None])
    grad_logits = ((probability - target_mask.astype(jnp.float32)) * upstream[:, None]).astype(jnp.bfloat16)
    grad_hidden = jnp.dot(grad_logits, head, preferred_element_type=jnp.float32).astype(jnp.bfloat16)
    blocks = jnp.transpose(grad_logits.reshape(TOKENS, N_VOCAB, V_DEV), (1, 0, 2))

    def head_block(grad_block):
        return lax.dot_general(grad_block, hidden, (((0,), (0,)), ((), ())), preferred_element_type=jnp.float32).astype(jnp.bfloat16)

    grad_head = lax.map(head_block, blocks).reshape(VOCAB, D)
    return token_loss, grad_hidden, grad_head
```

```python
import jax
import jax.numpy as jnp
from jax import lax
from jax.sharding import Mesh, PartitionSpec as P

X, Z, Y, C = 4, 16, 4, 2
VOCAB_AXES = ("x", "z")
ROW_AXES = ("y", "core")
SWAP = [(0, 1), (1, 0)]


def gather_over(block, axis):
    size = lax.axis_size(axis)
    copies = jnp.broadcast_to(block[None], (size,) + block.shape)
    return lax.all_to_all(copies, axis, 0, 0)


def pick(pair, index):
    return lax.dynamic_index_in_dim(pair, index, 1, keepdims=False)


def per_device(hidden, head, targets, upstream):
    width, slice_width = head.shape
    token_count = targets.shape[0]
    own = token_count // (Y * C)
    core = lax.axis_index("core")
    row_first = lax.axis_index(ROW_AXES) * own

    by_z = gather_over(hidden, "z").reshape(-1, slice_width)
    hidden_all = gather_over(by_z, "x").reshape(Y, C, own, slice_width)
    hidden_own = pick(hidden_all, core).reshape(-1, slice_width)
    hidden_other = pick(hidden_all, 1 - core).reshape(-1, slice_width)

    def logits_of(rows):
        return lax.dot_general(rows, head, (((1,), (1,)), ((), ())), preferred_element_type=jnp.float32)

    from_core = lax.ppermute(logits_of(hidden_other), "core", SWAP)
    chip_logits = (logits_of(hidden_own) + from_core).reshape(Y, own, width)
    logits = jnp.sum(lax.all_to_all(chip_logits, "y", 0, 0), axis=0)

    row_targets = lax.dynamic_slice_in_dim(targets, row_first, own, 0)
    row_weight = lax.dynamic_slice_in_dim(upstream, row_first, own, 0)
    columns = lax.broadcasted_iota(jnp.int32, logits.shape, 1) + lax.axis_index(VOCAB_AXES) * width
    target_mask = columns == row_targets[:, None]
    local_top = jnp.max(logits, axis=1)
    local_total = jnp.sum(jnp.exp(logits - local_top[:, None]), axis=1)
    local_target = jnp.sum(jnp.where(target_mask, logits, jnp.float32(0.0)), axis=1)
    stats = jnp.concatenate([local_top, local_total, local_target])
    stats = gather_over(stats[None], VOCAB_AXES).reshape(X * Z, 3, own)
    top = jnp.max(stats[:, 0], axis=0)
    total = jnp.sum(stats[:, 1] * jnp.exp(stats[:, 0] - top), axis=0)
    lse = top + jnp.log(total)
    token_loss = lse - jnp.sum(stats[:, 2], axis=0)
    probability = jnp.exp(logits - lse[:, None])
    grad_rows = ((probability - target_mask.astype(jnp.float32)) * row_weight[:, None]).astype(jnp.bfloat16)

    grad_own = gather_over(grad_rows, "y").reshape(Y * own, width)
    grad_other = lax.ppermute(grad_own, "core", SWAP)

    def partial_of(grad):
        return jnp.dot(grad, head, preferred_element_type=jnp.float32).astype(jnp.bfloat16).reshape(
            X, own, slice_width
        )

    partial = jnp.stack([partial_of(grad_own), partial_of(grad_other)], axis=1)
    over_x = jnp.sum(lax.all_to_all(partial, "x", 0, 0).astype(jnp.float32), axis=0).astype(jnp.bfloat16)
    over_x = jnp.where(core == 0, over_x, over_x[::-1]).reshape(Z, -1, slice_width)
    over_z = lax.all_to_all(over_x, "z", 0, 0)
    grad_hidden = jnp.sum(over_z.astype(jnp.float32), axis=0).astype(jnp.bfloat16)

    def head_part(grad, rows):
        return lax.dot_general(grad, rows, (((0,), (0,)), ((), ())), preferred_element_type=jnp.float32)

    grad_head = (head_part(grad_own, hidden_own) + head_part(grad_other, hidden_other)).astype(jnp.bfloat16)
    return token_loss, grad_hidden, grad_head


def solution(mesh):
    torus = Mesh(mesh.devices.reshape(X, Z, Y, C), VOCAB_AXES + ROW_AXES)
    return jax.shard_map(
        per_device,
        mesh=torus,
        in_specs=(P(VOCAB_AXES, ROW_AXES), P(VOCAB_AXES, ROW_AXES), P(), P()),
        out_specs=(P(ROW_AXES), P(VOCAB_AXES, ROW_AXES), P(VOCAB_AXES, ROW_AXES)),
        check_vma=False,
    )
```

```python
import jax
import jax.numpy as jnp
from jax import lax
from jax.sharding import Mesh, PartitionSpec as P

X, Z, Y, C = 4, 16, 4, 2
VOCAB_AXES = ("x", "z")
ROW_AXES = ("y", "core")
SWAP = [(0, 1), (1, 0)]


def gather_over(block, axis):
    size = lax.axis_size(axis)
    copies = jnp.broadcast_to(block[None], (size,) + block.shape)
    return lax.all_to_all(copies, axis, 0, 0)


def pick(pair, index):
    return lax.dynamic_index_in_dim(pair, index, 1, keepdims=False)


def per_device(hidden, head, targets, upstream):
    width, slice_width = head.shape
    token_count = targets.shape[0]
    own = token_count // (Y * C)
    core = lax.axis_index("core")
    row_first = lax.axis_index(ROW_AXES) * own

    head_other = lax.ppermute(head, "core", SWAP)

    by_z = gather_over(hidden, "z").reshape(1, C, own, slice_width)
    copies = jnp.broadcast_to(by_z, (X, C, own, slice_width)).reshape(X * C, own, slice_width)
    both = lax.all_to_all(copies, ("x", "core"), 0, 0).reshape(X, C, own, slice_width)
    hidden_own = pick(both, core).reshape(-1, slice_width)
    hidden_other = pick(both, 1 - core).reshape(-1, slice_width)

    def logits_of(rows, slice_of_head):
        return lax.dot_general(
            rows, slice_of_head, (((1,), (1,)), ((), ())), preferred_element_type=jnp.float32
        )

    chip_logits = (logits_of(hidden_own, head) + logits_of(hidden_other, head_other)).reshape(Y, own, width)
    logits = jnp.sum(lax.all_to_all(chip_logits, "y", 0, 0), axis=0)

    row_targets = lax.dynamic_slice_in_dim(targets, row_first, own, 0)
    row_weight = lax.dynamic_slice_in_dim(upstream, row_first, own, 0)
    columns = lax.broadcasted_iota(jnp.int32, logits.shape, 1) + lax.axis_index(VOCAB_AXES) * width
    target_mask = columns == row_targets[:, None]
    local_top = jnp.max(logits, axis=1)
    local_total = jnp.sum(jnp.exp(logits - local_top[:, None]), axis=1)
    local_target = jnp.sum(jnp.where(target_mask, logits, jnp.float32(0.0)), axis=1)
    stats = jnp.concatenate([local_top, local_total, local_target])
    stats = gather_over(stats[None], VOCAB_AXES).reshape(X * Z, 3, own)
    top = jnp.max(stats[:, 0], axis=0)
    total = jnp.sum(stats[:, 1] * jnp.exp(stats[:, 0] - top), axis=0)
    lse = top + jnp.log(total)
    token_loss = lse - jnp.sum(stats[:, 2], axis=0)
    probability = jnp.exp(logits - lse[:, None])
    grad_rows = ((probability - target_mask.astype(jnp.float32)) * row_weight[:, None]).astype(jnp.bfloat16)

    grad_half = gather_over(grad_rows, "y").reshape(Y * own, width)

    def partial_of(slice_of_head):
        return jnp.dot(grad_half, slice_of_head, preferred_element_type=jnp.float32).astype(jnp.bfloat16).reshape(
            X, own, slice_width
        )

    part_own, part_other = partial_of(head), partial_of(head_other)
    partial = jnp.stack(
        [jnp.where(core == 0, part_own, part_other), jnp.where(core == 0, part_other, part_own)], axis=1
    ).reshape(X * C, own, slice_width)
    over_x = lax.all_to_all(partial, ("x", "core"), 0, 0).reshape(X, C * own, slice_width)
    over_x = jnp.sum(over_x.astype(jnp.float32), axis=0).astype(jnp.bfloat16).reshape(Z, -1, slice_width)
    over_z = lax.all_to_all(over_x, "z", 0, 0)
    grad_hidden = jnp.sum(over_z.astype(jnp.float32), axis=0).astype(jnp.bfloat16)

    grad_rest = lax.ppermute(grad_half, "core", SWAP)
    hidden_rest = lax.ppermute(hidden_other, "core", SWAP)

    def head_part(grad, rows):
        return lax.dot_general(grad, rows, (((0,), (0,)), ((), ())), preferred_element_type=jnp.float32)

    grad_head = (head_part(grad_half, hidden_own) + head_part(grad_rest, hidden_rest)).astype(jnp.bfloat16)
    return token_loss, grad_hidden, grad_head


def solution(mesh):
    torus = Mesh(mesh.devices.reshape(X, Z, Y, C), VOCAB_AXES + ROW_AXES)
    return jax.shard_map(
        per_device,
        mesh=torus,
        in_specs=(P(VOCAB_AXES, ROW_AXES), P(VOCAB_AXES, ROW_AXES), P(), P()),
        out_specs=(P(ROW_AXES), P(VOCAB_AXES, ROW_AXES), P(VOCAB_AXES, ROW_AXES)),
        check_vma=False,
    )
```

```python
import jax
import jax.numpy as jnp
from jax import lax
from jax.experimental import pallas as pl
from jax.experimental.pallas import tpu as pltpu
from jax.sharding import Mesh, PartitionSpec as P

X, Z, Y, C = 4, 16, 4, 2
VOCAB_AXES = ("x", "z")
ROW_AXES = ("y", "core")
SWAP = [(0, 1), (1, 0)]
TILE = 256
BF16, F32 = jnp.bfloat16, jnp.float32
IN_VMEM = pl.BlockSpec(memory_space=pltpu.VMEM)
IN_SMEM = pl.BlockSpec(memory_space=pltpu.SMEM)


def call(kernel, out_shape, core_index, *operands):
    return pl.pallas_call(
        kernel,
        out_shape=out_shape,
        in_specs=[IN_SMEM] + [IN_VMEM] * len(operands),
        out_specs=IN_VMEM,
        compiler_params=pltpu.CompilerParams(vmem_limit_bytes=24 * 2**20),
    )(core_index, *operands)


def gather_over(block, axis):
    size = lax.axis_size(axis)
    copies = jnp.broadcast_to(block[None], (size,) + block.shape)
    return lax.all_to_all(copies, axis, 0, 0)


def logits_kernel(core_ref, rows_ref, head_ref, other_ref, out_ref):
    core = core_ref[0]
    slice_width = rows_ref.shape[-1]
    own = rows_ref[:, pl.ds(core, 1)].reshape(-1, slice_width)
    rest = rows_ref[:, pl.ds(1 - core, 1)].reshape(-1, slice_width)

    def dot(rows, part):
        return lax.dot_general(rows, part, (((1,), (1,)), ((), ())), preferred_element_type=F32)

    for first in range(0, head_ref.shape[0], TILE):
        span = pl.ds(first, TILE)
        tile = dot(own, head_ref[span, :]) + dot(rest, other_ref[span, :])
        out_ref[:, :, span] = tile.reshape(out_ref.shape[:2] + (TILE,))


def partial_kernel(core_ref, grad_ref, head_ref, other_ref, out_ref):
    core = core_ref[0]
    grad = grad_ref[...]
    blocks, _, own, slice_width = out_ref.shape
    for place, part in ((core, head_ref), (1 - core, other_ref)):
        for first in range(0, slice_width, TILE):
            span = pl.ds(first, TILE)
            tile = jnp.dot(grad, part[:, span], preferred_element_type=F32).astype(BF16)
            out_ref[:, pl.ds(place, 1), :, span] = tile.reshape(blocks, 1, own, TILE)


def per_device(hidden, head, targets, upstream):
    width, slice_width = head.shape
    token_count = targets.shape[0]
    own = token_count // (Y * C)
    padded = -(-width // TILE) * TILE
    core = lax.axis_index("core")
    core_index = core[None]
    row_first = lax.axis_index(ROW_AXES) * own

    head_other = lax.ppermute(head, "core", SWAP)
    pad = lambda a: jnp.pad(a, ((0, padded - width), (0, 0)))
    own_target = lax.dynamic_slice_in_dim(targets, row_first, own, 0) - lax.axis_index(VOCAB_AXES) * width
    own_weight = lax.dynamic_slice_in_dim(upstream, row_first, own, 0)

    by_z = gather_over(hidden, "z").reshape(1, C, own, slice_width)
    by_z, head, head_other, own_target, own_weight = lax.optimization_barrier(
        (by_z, pad(head), pad(head_other), own_target, own_weight)
    )
    copies = jnp.broadcast_to(by_z, (X, C, own, slice_width)).reshape(X * C, own, slice_width)
    both = lax.all_to_all(copies, ("x", "core"), 0, 0).reshape(X, C, own, slice_width)

    out = jax.ShapeDtypeStruct((Y, own, padded), F32)
    chip_logits = call(logits_kernel, out, core_index, both, head, head_other)
    logits = jnp.sum(lax.all_to_all(chip_logits, "y", 0, 0), axis=0)

    column = lax.broadcasted_iota(jnp.int32, logits.shape, 1)
    valid = column < width
    target_mask = (column == own_target[:, None]) & valid
    local_top = jnp.max(jnp.where(valid, logits, -jnp.inf), axis=1)
    local_total = jnp.sum(jnp.where(valid, jnp.exp(logits - local_top[:, None]), 0.0), axis=1)
    local_target = jnp.sum(jnp.where(target_mask, logits, 0.0), axis=1)
    stats = jnp.concatenate([local_top, local_total, local_target])
    stats = gather_over(stats[None], VOCAB_AXES).reshape(X * Z, 3, own)
    top = jnp.max(stats[:, 0], axis=0)
    total = jnp.sum(stats[:, 1] * jnp.exp(stats[:, 0] - top), axis=0)
    lse = top + jnp.log(total)
    token_loss = lse - jnp.sum(stats[:, 2], axis=0)
    probability = jnp.where(valid, jnp.exp(logits - lse[:, None]), 0.0)
    grad_rows = ((probability - target_mask.astype(F32)) * own_weight[:, None]).astype(BF16)

    grad_rows, token_loss = lax.optimization_barrier((grad_rows, token_loss))
    grad_half = gather_over(grad_rows, "y").reshape(Y * own, padded)

    out = jax.ShapeDtypeStruct((X, C, own, slice_width), BF16)
    partial = call(partial_kernel, out, core_index, grad_half, head, head_other)
    over_x = lax.all_to_all(partial.reshape(X * C, own, slice_width), ("x", "core"), 0, 0)
    over_x, both, grad_half = lax.optimization_barrier((over_x, both, grad_half))
    over_x = jnp.sum(over_x.reshape(X, C * own, slice_width).astype(F32), axis=0).astype(BF16)
    over_z = lax.all_to_all(over_x.reshape(Z, -1, slice_width), "z", 0, 0)
    grad_hidden = jnp.sum(over_z.astype(F32), axis=0).astype(BF16)

    pick = lambda index: lax.dynamic_index_in_dim(both, index, 1, keepdims=False).reshape(-1, slice_width)
    hidden_own, hidden_other = pick(core), pick(1 - core)
    grad_rest = lax.ppermute(grad_half, "core", SWAP)
    hidden_rest = lax.ppermute(hidden_other, "core", SWAP)

    def head_part(grad, rows):
        return lax.dot_general(grad[:, :width], rows, (((0,), (0,)), ((), ())), preferred_element_type=F32)

    grad_head = (head_part(grad_half, hidden_own) + head_part(grad_rest, hidden_rest)).astype(BF16)
    return token_loss, grad_hidden, grad_head


def solution(mesh):
    torus = Mesh(mesh.devices.reshape(X, Z, Y, C), VOCAB_AXES + ROW_AXES)
    return jax.shard_map(
        per_device,
        mesh=torus,
        in_specs=(P(VOCAB_AXES, ROW_AXES), P(VOCAB_AXES, ROW_AXES), P(), P()),
        out_specs=(P(ROW_AXES), P(VOCAB_AXES, ROW_AXES), P(VOCAB_AXES, ROW_AXES)),
        check_vma=False,
    )
```

```python
import jax
import jax.numpy as jnp
from jax import lax
from jax.experimental import pallas as pl
from jax.experimental.pallas import tpu as pltpu
from jax.sharding import Mesh, PartitionSpec as P

X, Z, Y, C = 4, 16, 4, 2
VOCAB_AXES = ("x", "z")
ROW_AXES = ("y", "core")
SWAP = [(0, 1), (1, 0)]
TILE = 256
LANES = 128
BF16, F32 = jnp.bfloat16, jnp.float32
IN_VMEM = pl.BlockSpec(memory_space=pltpu.VMEM)
IN_SMEM = pl.BlockSpec(memory_space=pltpu.SMEM)


def call(kernel, out_shape, flops, core_index, *operands):
    moved = sum(a.size * a.dtype.itemsize for a in operands) + out_shape.size * out_shape.dtype.itemsize
    return pl.pallas_call(
        kernel,
        out_shape=out_shape,
        in_specs=[IN_SMEM] + [IN_VMEM] * len(operands),
        out_specs=IN_VMEM,
        cost_estimate=pl.CostEstimate(flops=flops, bytes_accessed=moved, transcendentals=0),
        compiler_params=pltpu.CompilerParams(vmem_limit_bytes=8 * 2**20),
    )(core_index, *operands)


def gather_over(block, axis):
    size = lax.axis_size(axis)
    copies = jnp.broadcast_to(block[None], (size,) + block.shape)
    return lax.all_to_all(copies, axis, 0, 0)


def spans(length):
    return [pl.ds(first, min(TILE, length - first)) for first in range(0, length, TILE)]


def logits_kernel(core_ref, rows_ref, head_ref, other_ref, out_ref):
    core = core_ref[0]
    slice_width = rows_ref.shape[-1]
    own = rows_ref[:, pl.ds(core, 1)].reshape(-1, slice_width)
    rest = rows_ref[:, pl.ds(1 - core, 1)].reshape(-1, slice_width)

    def dot(rows, part):
        return lax.dot_general(rows, part, (((1,), (1,)), ((), ())), preferred_element_type=F32)

    for span in spans(head_ref.shape[0]):
        tile = dot(own, head_ref[span, :]) + dot(rest, other_ref[span, :])
        out_ref[:, :, span] = tile.reshape(out_ref.shape[:2] + (span.size,))


def partial_kernel(core_ref, weight_ref, head_ref, other_ref, out_ref):
    core = core_ref[0]
    blocks, _, own, slice_width = out_ref.shape
    weight = weight_ref[:, : head_ref.shape[0]]
    for place, part in ((core, head_ref), (1 - core, other_ref)):
        for span in spans(slice_width):
            tile = jnp.dot(weight, part[:, span], preferred_element_type=F32).astype(BF16)
            out_ref[:, pl.ds(place, 1), :, span] = tile.reshape(blocks, 1, own, span.size)


def to_pieces(columns):
    pieces = []
    for column in columns:
        for _ in range(3):
            piece = lax.reduce_precision(column, 8, 7)
            pieces.append(piece.astype(BF16))
            column = column - piece
    return jnp.stack(pieces, axis=1)


def from_pieces(pieces):
    return jnp.sum(pieces.astype(F32).reshape(pieces.shape[:-1] + (-1, 3)), axis=-1)


def halve(rows, axis, bit):
    size = lax.axis_size(axis)
    mine = (lax.axis_index(axis) >> bit) & 1
    pair = rows.reshape((2, -1) + rows.shape[1:])
    keep, send = (lax.dynamic_index_in_dim(pair, k, 0, keepdims=False) for k in (mine, 1 - mine))
    return keep + lax.ppermute(send, axis, [(i, i ^ (1 << bit)) for i in range(size)])


def per_device(hidden, head, targets, upstream):
    width, slice_width = head.shape
    block = hidden.shape[0]
    token_count = targets.shape[0]
    own = token_count // (Y * C)
    padded = -(-width // LANES) * LANES
    core = lax.axis_index("core")
    core_index = core[None]
    row_first = lax.axis_index(ROW_AXES) * own
    block_first = lax.axis_index(VOCAB_AXES) * block
    chunk_first = lax.axis_index("x") * block * Z
    barrier = lax.optimization_barrier

    def in_core_order(mine, other, axis):
        return jnp.where(core == 0, jnp.stack([mine, other], axis), jnp.stack([other, mine], axis))

    by_z = gather_over(hidden, "z").reshape(1, C, own, slice_width)
    head_other = lax.ppermute(head, "core", SWAP)
    local_targets = targets - lax.axis_index(VOCAB_AXES) * width
    own_target = lax.dynamic_slice_in_dim(local_targets, row_first, own, 0)
    block_weight = lax.dynamic_slice_in_dim(upstream, block_first, block, 0)
    pick_target = local_targets[:, None] == lax.broadcasted_iota(jnp.int32, (token_count, width), 1)
    target_rows = jnp.dot(pick_target.astype(BF16), head, preferred_element_type=F32).astype(BF16)
    target_rows = halve(target_rows, "x", 1)
    by_z, head_other, own_target, block_weight, target_rows = barrier(
        (by_z, head_other, own_target, block_weight, target_rows)
    )

    copies = jnp.broadcast_to(by_z, (X, C, own, slice_width)).reshape(X * C, own, slice_width)
    both = lax.all_to_all(copies, ("x", "core"), 0, 0).reshape(X, C, own, slice_width)
    target_rows = halve(target_rows, "x", 0)
    both, target_rows = barrier((both, target_rows))

    out = jax.ShapeDtypeStruct((Y, own, width), F32)
    flops = 4 * Y * own * width * slice_width
    chip_logits = call(logits_kernel, out, flops, core_index, both, head, head_other)
    logit_parts = lax.all_to_all(chip_logits, "y", 0, 0)
    target_rows = halve(target_rows, "z", 3)
    logit_parts, target_rows = barrier((logit_parts, target_rows))
    logits = jnp.sum(logit_parts, axis=0)

    target_mask = lax.broadcasted_iota(jnp.int32, logits.shape, 1) == own_target[:, None]
    top = jnp.max(logits, axis=1)
    weight = jnp.exp(logits - top[:, None])
    total = jnp.sum(weight, axis=1)
    target_logit = jnp.sum(jnp.where(target_mask, logits, 0.0), axis=1)
    weight = jnp.where(target_mask, 0.0, weight).astype(BF16)
    tail = to_pieces([top, total, target_logit])
    tail = jnp.pad(tail, ((0, 0), (0, padded - width - tail.shape[1])))
    weights = gather_over(jnp.concatenate([weight, tail], axis=1), "y")
    target_rows = halve(target_rows, "z", 2)
    weights, target_rows = barrier((weights, target_rows))
    weights = weights.reshape(Y * own, padded)

    out = jax.ShapeDtypeStruct((X, C, own, slice_width), BF16)
    partial = call(partial_kernel, out, flops, core_index, weights, head, head_other)
    over_x = lax.all_to_all(partial.reshape(X * C, own, slice_width), ("x", "core"), 0, 0)
    over_x = over_x.reshape(X, C * own, slice_width)
    target_rows = halve(target_rows, "z", 1)

    weights_rest = lax.ppermute(weights, "core", SWAP)
    read = lambda w: from_pieces(w[:, width : width + 9]).reshape(Y, own, 3)
    stats = in_core_order(read(weights), read(weights_rest), 1).reshape(token_count, 3).T
    by_x = lax.all_gather(stats, "x")
    x_top = jnp.max(by_x[:, 0], axis=0)
    x_scale = jnp.exp(by_x[:, 0] - x_top)
    x_stats = jnp.stack([x_top, jnp.sum(x_scale * by_x[:, 1], axis=0), jnp.sum(by_x[:, 2], axis=0)])
    scale = lax.dynamic_slice_in_dim(x_scale, chunk_first, C * own, 1)
    over_x, target_rows, scale = barrier((over_x, target_rows, scale))
    over_x = jnp.sum(over_x.astype(F32) * scale[:, :, None], axis=0).astype(BF16)

    over_z = lax.all_to_all(over_x.reshape(Z, block, slice_width), "z", 0, 0)
    target_rows = halve(target_rows, "z", 0)
    by_z_stats = lax.all_gather(x_stats, "z")
    z_top = jnp.max(by_z_stats[:, 0], axis=0)
    z_scale = jnp.exp(by_z_stats[:, 0] - z_top)
    all_total = jnp.sum(z_scale * by_z_stats[:, 1], axis=0)
    all_target = jnp.sum(by_z_stats[:, 2], axis=0)
    lse = z_top + jnp.log(all_total)
    loss = lse - all_target
    target_grad = jnp.exp(-loss) - 1.0
    of_block = lambda a: lax.dynamic_slice_in_dim(a, block_first, block, a.ndim - 1)
    scale = of_block(z_scale / all_total)[:, :, None]
    grad_hidden = jnp.sum(over_z.astype(F32) * scale, axis=0)
    grad_hidden = grad_hidden + of_block(target_grad)[:, None] * target_rows.astype(F32)
    grad_hidden = (grad_hidden * block_weight[:, None]).astype(BF16)
    token_loss = lax.dynamic_slice_in_dim(loss, row_first, own, 0)

    by_half = lambda a, half: lax.dynamic_index_in_dim(a.reshape(Y, C, own), half, 1, keepdims=False).reshape(-1)
    pick = lambda half: lax.dynamic_index_in_dim(both, half, 1, keepdims=False).reshape(-1, slice_width)
    hidden_rest = lax.ppermute(pick(1 - core), "core", SWAP)
    row_scale = jnp.exp(stats[0] - lse) * upstream
    row_target = target_grad * upstream

    def head_part(half, weights, rows):
        grad = weights[:, :width].astype(F32) * by_half(row_scale, half)[:, None]
        column = lax.broadcasted_iota(jnp.int32, grad.shape, 1)
        at_target = column == by_half(local_targets, half)[:, None]
        grad = jnp.where(at_target, by_half(row_target, half)[:, None], grad).astype(BF16)
        return lax.dot_general(grad, rows, (((0,), (0,)), ((), ())), preferred_element_type=F32)

    grad_head = head_part(core, weights, pick(core)) + head_part(1 - core, weights_rest, hidden_rest)
    return token_loss, grad_hidden, grad_head.astype(BF16)


def solution(mesh):
    torus = Mesh(mesh.devices.reshape(X, Z, Y, C), VOCAB_AXES + ROW_AXES)
    return jax.shard_map(
        per_device,
        mesh=torus,
        in_specs=(P(VOCAB_AXES, ROW_AXES), P(VOCAB_AXES, ROW_AXES), P(), P()),
        out_specs=(P(ROW_AXES), P(VOCAB_AXES, ROW_AXES), P(VOCAB_AXES, ROW_AXES)),
        check_vma=False,
    )
```

```python
import jax
import jax.numpy as jnp
from jax import lax
from jax.experimental import pallas as pl
from jax.experimental.pallas import tpu as pltpu
from jax.sharding import Mesh, PartitionSpec as P

X, Z, Y, C = 4, 16, 4, 2
VOCAB_AXES = ("x", "z")
ROW_AXES = ("y", "core")
SWAP = [(0, 1), (1, 0)]
TILE = 256
BF16, F32 = jnp.bfloat16, jnp.float32
IN_VMEM = pl.BlockSpec(memory_space=pltpu.VMEM)
IN_SMEM = pl.BlockSpec(memory_space=pltpu.SMEM)


def call(kernel, out_shape, core_index, rows, head, other):
    moved = sum(a.size * a.dtype.itemsize for a in (rows, head, other, out_shape))
    flops = rows.size * head.shape[0] * 2
    return pl.pallas_call(
        kernel,
        out_shape=out_shape,
        in_specs=[IN_SMEM] + [IN_VMEM] * 3,
        out_specs=IN_VMEM,
        scratch_shapes=[pltpu.VMEM((C, TILE, head.shape[1]), BF16)],
        cost_estimate=pl.CostEstimate(flops=flops, bytes_accessed=moved, transcendentals=0),
        compiler_params=pltpu.CompilerParams(vmem_limit_bytes=8 * 2**20),
    )(core_index, rows, head, other)


def gather_over(block, axis):
    size = lax.axis_size(axis)
    copies = jnp.broadcast_to(block[None], (size,) + block.shape)
    return lax.all_to_all(copies, axis, 0, 0)


def pad_last_rows(tail_ref, head_ref):
    rest = head_ref.shape[0] % TILE
    tail_ref[...] = jnp.zeros_like(tail_ref)
    tail_ref[:rest, :] = head_ref[head_ref.shape[0] - rest :, :]


def logits_kernel(core_ref, rows_ref, head_ref, other_ref, out_ref, tail_ref):
    core = core_ref[0]
    slice_width = rows_ref.shape[-1]
    own = rows_ref[:, pl.ds(core, 1)].reshape(-1, slice_width)
    rest = rows_ref[:, pl.ds(1 - core, 1)].reshape(-1, slice_width)
    pad_last_rows(tail_ref.at[0], head_ref)
    pad_last_rows(tail_ref.at[1], other_ref)

    def dot(rows, part):
        return lax.dot_general(rows, part, (((1,), (1,)), ((), ())), preferred_element_type=F32)

    whole = head_ref.shape[0] // TILE
    for k in range(whole + 1):
        span = pl.ds(k * TILE, TILE)
        part, other = (head_ref[span, :], other_ref[span, :]) if k < whole else (tail_ref[0], tail_ref[1])
        tile = dot(own, part) + dot(rest, other)
        out_ref[:, :, span] = tile.reshape(out_ref.shape[:2] + (TILE,))


def partial_kernel(core_ref, grad_ref, head_ref, other_ref, out_ref, tail_ref):
    core = core_ref[0]
    blocks, _, own, slice_width = out_ref.shape
    whole = head_ref.shape[0] // TILE * TILE
    grad, grad_tail = grad_ref[:, :whole], grad_ref[:, whole:]
    for k, (place, part) in enumerate(((core, head_ref), (1 - core, other_ref))):
        pad_last_rows(tail_ref.at[k], part)
        for first in range(0, slice_width, TILE):
            span = pl.ds(first, TILE)
            tile = jnp.dot(grad, part[:whole, span], preferred_element_type=F32)
            tile = tile + jnp.dot(grad_tail, tail_ref[k, :, span], preferred_element_type=F32)
            out_ref[:, pl.ds(place, 1), :, span] = tile.astype(BF16).reshape(blocks, 1, own, TILE)


def per_device(hidden, head, targets, upstream):
    width, slice_width = head.shape
    token_count = targets.shape[0]
    own = token_count // (Y * C)
    padded = -(-width // TILE) * TILE
    barrier = lax.optimization_barrier

    by_z = gather_over(hidden, "z").reshape(1, C, own, slice_width)
    core = lax.axis_index("core")
    row_first = lax.axis_index(ROW_AXES) * own
    own_target = lax.dynamic_slice_in_dim(targets, row_first, own, 0) - lax.axis_index(VOCAB_AXES) * width
    own_weight = lax.dynamic_slice_in_dim(upstream, row_first, own, 0)
    column = lax.broadcasted_iota(jnp.int32, (own, padded), 1)
    valid = jnp.where(column < width, 1.0, 0.0)
    target_mask = jnp.where(column == own_target[:, None], valid, 0.0)
    head, own_weight, target_mask, valid = barrier((head, own_weight, target_mask, valid))
    head_other = lax.ppermute(head, "core", SWAP)
    by_z, own_weight, target_mask, valid, core = barrier((by_z, own_weight, target_mask, valid, core))
    core_index = core[None]

    copies = jnp.broadcast_to(by_z, (X, C, own, slice_width)).reshape(X * C, own, slice_width)
    both = lax.all_to_all(copies, ("x", "core"), 0, 0).reshape(X, C, own, slice_width)

    out = jax.ShapeDtypeStruct((Y, own, padded), F32)
    chip_logits = call(logits_kernel, out, core_index, both, head, head_other)
    logit_parts = lax.all_to_all(chip_logits, "y", 0, 0)
    logit_parts, own_weight, target_mask, valid, core = barrier((logit_parts, own_weight, target_mask, valid, core))
    logits = jnp.sum(logit_parts, axis=0)

    local_top = jnp.max(jnp.where(valid > 0, logits, -jnp.inf), axis=1)
    local_total = jnp.sum(jnp.where(valid > 0, jnp.exp(logits - local_top[:, None]), 0.0), axis=1)
    local_target = jnp.sum(jnp.where(target_mask > 0, logits, 0.0), axis=1)
    stats = jnp.concatenate([local_top, local_total, local_target])
    stats = gather_over(stats[None], VOCAB_AXES).reshape(X * Z, 3, own)
    stats, logits, own_weight, target_mask, valid = barrier((stats, logits, own_weight, target_mask, valid))
    top = jnp.max(stats[:, 0], axis=0)
    total = jnp.sum(stats[:, 1] * jnp.exp(stats[:, 0] - top), axis=0)
    lse = top + jnp.log(total)
    token_loss = lse - jnp.sum(stats[:, 2], axis=0)
    probability = jnp.where(valid > 0, jnp.exp(logits - lse[:, None]), 0.0)
    grad_rows = ((probability - target_mask) * own_weight[:, None]).astype(BF16)

    grad_rows, token_loss = barrier((grad_rows, token_loss))
    grad_half = gather_over(grad_rows, "y").reshape(Y * own, padded)

    grad_half, core = barrier((grad_half, core))
    out = jax.ShapeDtypeStruct((X, C, own, slice_width), BF16)
    partial = call(partial_kernel, out, core_index, grad_half, head, head_other)
    over_x = lax.all_to_all(partial.reshape(X * C, own, slice_width), ("x", "core"), 0, 0)
    over_x, both, grad_half, core = barrier((over_x, both, grad_half, core))
    over_x = jnp.sum(over_x.reshape(X, C * own, slice_width).astype(F32), axis=0).astype(BF16)
    over_z = lax.all_to_all(over_x.reshape(Z, -1, slice_width), "z", 0, 0)
    grad_hidden = jnp.sum(over_z.astype(F32), axis=0).astype(BF16)

    def head_part(grad, rows):
        return lax.dot_general(grad[:, :width], rows, (((0,), (0,)), ((), ())), preferred_element_type=F32)

    pick = lambda index: lax.dynamic_index_in_dim(both, index, 1, keepdims=False).reshape(-1, slice_width)
    part = head_part(grad_half, pick(core))
    part, grad_half, both = barrier((part, grad_half, both))
    grad_rest = lax.ppermute(grad_half, "core", SWAP)
    hidden_rest = lax.ppermute(pick(1 - core), "core", SWAP)
    grad_head = (part + head_part(grad_rest, hidden_rest)).astype(BF16)
    return token_loss, grad_hidden, grad_head


def solution(mesh):
    torus = Mesh(mesh.devices.reshape(X, Z, Y, C), VOCAB_AXES + ROW_AXES)
    return jax.shard_map(
        per_device,
        mesh=torus,
        in_specs=(P(VOCAB_AXES, ROW_AXES), P(VOCAB_AXES, ROW_AXES), P(), P()),
        out_specs=(P(ROW_AXES), P(VOCAB_AXES, ROW_AXES), P(VOCAB_AXES, ROW_AXES)),
        check_vma=False,
    )
```

```python
import functools

import jax
import jax.numpy as jnp
from jax import lax
from jax.experimental import pallas as pl
from jax.experimental.pallas import tpu as pltpu
from jax.sharding import Mesh, PartitionSpec as P

X, Z, Y, C = 4, 16, 4, 2
VOCAB_AXES = ("x", "z")
ROW_AXES = ("y", "core")
SWAP = [(0, 1), (1, 0)]
LANES = 128
TILE = 256
BF16, F32 = jnp.bfloat16, jnp.float32
IN_VMEM = pl.BlockSpec(memory_space=pltpu.VMEM)
IN_SMEM = pl.BlockSpec(memory_space=pltpu.SMEM)


def call(kernel, out_shape, place, *operands, aliases=None):
    many = isinstance(out_shape, list)
    moved = sum(a.size * a.dtype.itemsize for a in operands)
    return pl.pallas_call(
        kernel,
        out_shape=out_shape,
        in_specs=[IN_SMEM] + [IN_VMEM] * len(operands),
        out_specs=[IN_VMEM] * len(out_shape) if many else IN_VMEM,
        input_output_aliases=aliases or {},
        cost_estimate=pl.CostEstimate(flops=moved, bytes_accessed=moved, transcendentals=0),
        compiler_params=pltpu.CompilerParams(vmem_limit_bytes=8 * 2**20),
    )(place, *operands)


def gather_over(block, axis):
    size = lax.axis_size(axis)
    copies = jnp.broadcast_to(block[None], (size,) + block.shape)
    return lax.all_to_all(copies, axis, 0, 0)


def to_lanes(column):
    shape = (column.shape[0], LANES)
    row, lane = (lax.broadcasted_iota(jnp.int32, shape, axis) for axis in (0, 1))
    return jnp.sum(jnp.where(row == lane, column, 0.0), axis=0, keepdims=True)


def to_column(lanes, rows, first=0):
    shape = (rows, lanes.shape[1])
    row, lane = (lax.broadcasted_iota(jnp.int32, shape, axis) for axis in (0, 1))
    return jnp.sum(jnp.where(row + first == lane, lanes, jnp.zeros_like(lanes)), axis=1, keepdims=True)


def target_mask(place_ref, targets_ref, shape):
    column = to_column(targets_ref[...], shape[0], place_ref[1]) - place_ref[2]
    return lax.broadcasted_iota(jnp.int32, shape, 1) == column


def spans(length):
    return [pl.ds(first, min(TILE, length - first)) for first in range(0, length, TILE)]


def logits_kernel(shift, place_ref, rows_ref, head_ref, out_ref):
    half = pl.ds(lax.rem(place_ref[0] + shift, C), 1)
    rows = rows_ref[:, half].reshape(-1, rows_ref.shape[-1])
    for span in spans(head_ref.shape[0]):
        tile = lax.dot_general(rows, head_ref[span, :], (((1,), (1,)), ((), ())), preferred_element_type=F32)
        out_ref[:, :, span] = tile.reshape(out_ref.shape[:2] + (span.size,))


def add_kernel(place_ref, a_ref, b_ref, out_ref):
    out_ref[...] = a_ref[...] + b_ref[...]


def partial_kernel(half, place_ref, grad_ref, head_ref, *refs):
    out_ref = refs[-1]
    blocks, _, own, slice_width = out_ref.shape
    grad = grad_ref[...].reshape(blocks * own, -1)
    for span in spans(slice_width):
        tile = jnp.dot(grad, head_ref[:, span], preferred_element_type=F32).astype(BF16)
        out_ref[:, half, :, span] = tile.reshape(blocks, own, span.size)


def statistics_kernel(place_ref, parts_ref, targets_ref, logits_ref, stats_ref):
    logits = parts_ref[0]
    for y in range(1, Y):
        logits = logits + parts_ref[y]
    logits_ref[...] = logits
    top = jnp.max(logits, axis=1, keepdims=True)
    total = jnp.sum(jnp.exp(logits - top), axis=1, keepdims=True)
    mask = target_mask(place_ref, targets_ref, logits.shape)
    target_logit = jnp.sum(jnp.where(mask, logits, 0.0), axis=1, keepdims=True)
    row = jnp.concatenate([to_lanes(a) for a in (top, total, target_logit)], axis=1)
    stats_ref[...] = jnp.broadcast_to(row[None], stats_ref.shape)


def softmax_kernel(place_ref, stats_ref, logits_ref, targets_ref, upstream_ref, loss_ref, grad_ref):
    logits = logits_ref[...]
    rows = logits.shape[0]
    stats = stats_ref[:, 0, :]
    tops, totals, target_logits = (stats[:, k * LANES : (k + 1) * LANES] for k in range(3))
    top = jnp.max(tops, axis=0, keepdims=True)
    total = jnp.sum(totals * jnp.exp(tops - top), axis=0, keepdims=True)
    used = lax.broadcasted_iota(jnp.int32, top.shape, 1) < rows
    lse = top + jnp.log(jnp.where(used, total, 1.0))
    loss = lse - jnp.sum(target_logits, axis=0, keepdims=True)
    loss_ref[...] = loss[:, :rows]
    weight = to_column(upstream_ref[...], rows, place_ref[1])
    mask = target_mask(place_ref, targets_ref, logits.shape)
    probability = jnp.exp(logits - to_column(lse, rows))
    grad = ((probability - jnp.where(mask, 1.0, 0.0)) * weight).astype(BF16)
    grad_ref[...] = jnp.broadcast_to(grad[None], grad_ref.shape)


def over_x_kernel(place_ref, parts_ref, out_ref):
    core = place_ref[0]
    blocks, block, _ = out_ref.shape
    per_half = blocks // C
    for half in range(C):
        where = pl.ds(lax.rem(core + half, C), 1)
        rows = parts_ref[0, where][0].astype(F32)
        for x in range(1, X):
            rows = rows + parts_ref[x, where][0].astype(F32)
        for k in range(per_half):
            out_ref[half * per_half + k] = rows[k * block : (k + 1) * block].astype(BF16)


def per_device(hidden, head, targets, upstream):
    width, slice_width = head.shape
    token_count = targets.shape[0]
    own = token_count // (Y * C)
    barrier = lax.optimization_barrier

    core = lax.axis_index("core")
    row_first = lax.axis_index(ROW_AXES) * own
    first_column = lax.axis_index(VOCAB_AXES) * width
    hidden, core, row_first, first_column = barrier((hidden, core, row_first, first_column))
    by_z = gather_over(hidden, "z").reshape(-1, slice_width)
    by_x = gather_over(by_z, "x").reshape(Y, C, own, slice_width)

    by_x, targets, upstream, core, row_first, first_column = barrier(
        (by_x, targets, upstream, core, row_first, first_column)
    )
    place = jnp.stack([core, row_first, first_column])
    out = jax.ShapeDtypeStruct((Y, own, width), F32)
    sibling_logits = call(functools.partial(logits_kernel, 1), out, place, by_x, head)
    from_core = lax.ppermute(sibling_logits, "core", SWAP)
    sibling_logits, targets, upstream, by_x = barrier((sibling_logits, targets, upstream, by_x))
    own_logits = call(functools.partial(logits_kernel, 0), out, place, by_x, head)
    chip_logits = call(add_kernel, out, place, own_logits, from_core)
    chip_logits, targets, upstream = barrier((chip_logits, targets[None], upstream[None]))
    parts = lax.all_to_all(chip_logits, "y", 0, 0)

    out = [jax.ShapeDtypeStruct((own, width), F32), jax.ShapeDtypeStruct((X * Z, 1, 3 * LANES), F32)]
    logits, stats = call(statistics_kernel, out, place, parts, targets)
    stats = lax.all_to_all(stats, VOCAB_AXES, 0, 0)
    out = [jax.ShapeDtypeStruct((1, own), F32), jax.ShapeDtypeStruct((Y, own, width), BF16)]
    token_loss, grad_rows = call(softmax_kernel, out, place, stats, logits, targets, upstream)

    grad_own = lax.all_to_all(grad_rows, "y", 0, 0)
    grad_other = lax.ppermute(grad_own, "core", SWAP)

    out = jax.ShapeDtypeStruct((X, C, own, slice_width), BF16)
    partial = call(functools.partial(partial_kernel, 0), out, place, grad_own, head)
    partial = call(functools.partial(partial_kernel, 1), out, place, grad_other, head, partial, aliases={3: 0})
    over_x = lax.all_to_all(partial, "x", 0, 0)
    over_x, place, by_x, core, grad_own, grad_other = barrier((over_x, place, by_x, core, grad_own, grad_other))
    out = jax.ShapeDtypeStruct((Z, token_count // (X * Z), slice_width), BF16)
    over_x = call(over_x_kernel, out, place, over_x)
    over_z = lax.all_to_all(over_x, "z", 0, 0)
    grad_hidden = jnp.sum(over_z.astype(F32), axis=0).astype(BF16)

    def head_part(grad, half):
        rows = lax.dynamic_index_in_dim(by_x, half, 1, keepdims=False).reshape(-1, slice_width)
        grad = grad.reshape(-1, width)
        return lax.dot_general(grad, rows, (((0,), (0,)), ((), ())), preferred_element_type=F32)

    grad_head = (head_part(grad_own, core) + head_part(grad_other, 1 - core)).astype(BF16)
    return token_loss[0], grad_hidden, grad_head


def solution(mesh):
    torus = Mesh(mesh.devices.reshape(X, Z, Y, C), VOCAB_AXES + ROW_AXES)
    return jax.shard_map(
        per_device,
        mesh=torus,
        in_specs=(P(VOCAB_AXES, ROW_AXES), P(VOCAB_AXES, ROW_AXES), P(), P()),
        out_specs=(P(ROW_AXES), P(VOCAB_AXES, ROW_AXES), P(VOCAB_AXES, ROW_AXES)),
        check_vma=False,
    )
```

```python
import functools

import jax
import jax.numpy as jnp
from jax import lax
from jax.experimental import pallas as pl
from jax.experimental.pallas import tpu as pltpu
from jax.sharding import Mesh, PartitionSpec as P

X, Z, Y, C = 4, 16, 4, 2
VOCAB_AXES = ("x", "z")
ROW_AXES = ("y", "core")
SWAP = [(0, 1), (1, 0)]
LANES = 128
TILE = 256
BF16, F32 = jnp.bfloat16, jnp.float32
IN_VMEM = pl.BlockSpec(memory_space=pltpu.VMEM)
IN_SMEM = pl.BlockSpec(memory_space=pltpu.SMEM)


def call(kernel, out_shape, place, *operands, aliases=None):
    many = isinstance(out_shape, list)
    moved = sum(a.size * a.dtype.itemsize for a in operands)
    return pl.pallas_call(
        kernel,
        out_shape=out_shape,
        in_specs=[IN_SMEM] + [IN_VMEM] * len(operands),
        out_specs=[IN_VMEM] * len(out_shape) if many else IN_VMEM,
        input_output_aliases=aliases or {},
        cost_estimate=pl.CostEstimate(flops=moved, bytes_accessed=moved, transcendentals=0),
        compiler_params=pltpu.CompilerParams(vmem_limit_bytes=8 * 2**20),
    )(place, *operands)


def gather_over(block, axis):
    size = lax.axis_size(axis)
    copies = jnp.broadcast_to(block[None], (size,) + block.shape)
    return lax.all_to_all(copies, axis, 0, 0)


def to_lanes(column, first):
    shape = (column.shape[0], LANES)
    row, lane = (lax.broadcasted_iota(jnp.int32, shape, axis) for axis in (0, 1))
    return jnp.sum(jnp.where(row + first == lane, column, 0.0), axis=0, keepdims=True)


def to_column(lanes, rows, first=0):
    shape = (rows, lanes.shape[1])
    row, lane = (lax.broadcasted_iota(jnp.int32, shape, axis) for axis in (0, 1))
    return jnp.sum(jnp.where(row + first == lane, lanes, jnp.zeros_like(lanes)), axis=1, keepdims=True)


def target_mask(place_ref, targets_ref, shape):
    column = to_column(targets_ref[...], shape[0], place_ref[1]) - place_ref[2]
    return lax.broadcasted_iota(jnp.int32, shape, 1) == column


def spans(length):
    return [pl.ds(first, min(TILE, length - first)) for first in range(0, length, TILE)]


def logits_kernel(shift, place_ref, rows_ref, head_ref, out_ref):
    half = pl.ds(lax.rem(place_ref[0] + shift, C), 1)
    rows = rows_ref[:, half].reshape(-1, rows_ref.shape[-1])
    for span in spans(head_ref.shape[0]):
        tile = lax.dot_general(rows, head_ref[span, :], (((1,), (1,)), ((), ())), preferred_element_type=F32)
        out_ref[:, :, span] = tile.reshape(out_ref.shape[:2] + (span.size,))


def add_kernel(place_ref, a_ref, b_ref, out_ref):
    out_ref[...] = a_ref[...] + b_ref[...]


def partial_kernel(half, place_ref, grad_ref, head_ref, *refs):
    out_ref = refs[-1]
    blocks, _, own, slice_width = out_ref.shape
    grad = grad_ref[...].reshape(blocks * own, -1)
    for span in spans(slice_width):
        tile = jnp.dot(grad, head_ref[:, span], preferred_element_type=F32).astype(BF16)
        out_ref[:, half, :, span] = tile.reshape(blocks, own, span.size)


def statistics_kernel(place_ref, parts_ref, targets_ref, logits_ref, stats_ref):
    logits = parts_ref[0]
    for y in range(1, Y):
        logits = logits + parts_ref[y]
    logits_ref[...] = logits
    top = jnp.max(logits, axis=1, keepdims=True)
    total = jnp.sum(jnp.exp(logits - top), axis=1, keepdims=True)
    mask = target_mask(place_ref, targets_ref, logits.shape)
    target_logit = jnp.sum(jnp.where(mask, logits, 0.0), axis=1, keepdims=True)
    row = to_lanes(top + jnp.log(total), 0) + to_lanes(target_logit, LANES // 2)
    stats_ref[...] = jnp.broadcast_to(row[None], stats_ref.shape)


def softmax_kernel(place_ref, stats_ref, logits_ref, targets_ref, upstream_ref, loss_ref, grad_ref):
    logits = logits_ref[...]
    rows = logits.shape[0]
    stats = stats_ref[:, 0, :]
    top = jnp.max(stats, axis=0, keepdims=True)
    lse = to_column(top + jnp.log(jnp.sum(jnp.exp(stats - top), axis=0, keepdims=True)), rows)
    target_logit = to_column(jnp.sum(stats, axis=0, keepdims=True), rows, LANES // 2)
    loss_ref[...] = to_lanes(lse - target_logit, 0)[:, :rows]
    weight = to_column(upstream_ref[...], rows, place_ref[1])
    mask = target_mask(place_ref, targets_ref, logits.shape)
    probability = jnp.exp(logits - lse)
    grad = ((probability - jnp.where(mask, 1.0, 0.0)) * weight).astype(BF16)
    grad_ref[...] = jnp.broadcast_to(grad[None], grad_ref.shape)


def over_x_kernel(place_ref, parts_ref, out_ref):
    core = place_ref[0]
    slice_width = parts_ref.shape[-1]
    blocks, pieces, _ = out_ref.shape
    block = out_ref.shape[2] // slice_width
    per_half = blocks // C
    for half in range(C):
        where = pl.ds(lax.rem(core + half, C), 1)
        rows = parts_ref[0, where][0].astype(F32)
        for x in range(1, X):
            rows = rows + parts_ref[x, where][0].astype(F32)
        for k in range(per_half):
            for part in range(pieces):
                for row in range(block):
                    first = k * pieces * block + part * block + row
                    span = pl.ds(row * slice_width, slice_width)
                    out_ref[half * per_half + k, part : part + 1, span] = rows[first : first + 1].astype(BF16)


def per_device(hidden, head, targets, upstream):
    width, slice_width = head.shape
    token_count = targets.shape[0]
    own = token_count // (Y * C)
    barrier = lax.optimization_barrier

    core = lax.axis_index("core")
    row_first = lax.axis_index(ROW_AXES) * own
    first_column = lax.axis_index(VOCAB_AXES) * width
    hidden, core, row_first, first_column = barrier((hidden, core, row_first, first_column))
    by_z = gather_over(hidden.reshape(2, -1), "z").reshape(-1, slice_width)
    by_x = gather_over(by_z, "x").reshape(Y, C, own, slice_width)

    by_x, targets, upstream, core, row_first, first_column = barrier(
        (by_x, targets, upstream, core, row_first, first_column)
    )
    place = jnp.stack([core, row_first, first_column])
    out = jax.ShapeDtypeStruct((Y, own, width), F32)
    sibling_logits = call(functools.partial(logits_kernel, 1), out, place, by_x, head)
    from_core = lax.ppermute(sibling_logits, "core", SWAP)
    sibling_logits, targets, upstream, by_x = barrier((sibling_logits, targets, upstream, by_x))
    own_logits = call(functools.partial(logits_kernel, 0), out, place, by_x, head)
    chip_logits = call(add_kernel, out, place, own_logits, from_core)
    chip_logits, targets, upstream = barrier((chip_logits, targets[None], upstream[None]))
    parts = lax.all_to_all(chip_logits, "y", 0, 0)

    out = [jax.ShapeDtypeStruct((own, width), F32), jax.ShapeDtypeStruct((X * Z, 1, LANES), F32)]
    logits, stats = call(statistics_kernel, out, place, parts, targets)
    stats = lax.all_to_all(stats, VOCAB_AXES, 0, 0)
    out = [jax.ShapeDtypeStruct((1, own), F32), jax.ShapeDtypeStruct((Y, own, width), BF16)]
    token_loss, grad_rows = call(softmax_kernel, out, place, stats, logits, targets, upstream)

    grad_own = lax.all_to_all(grad_rows, "y", 0, 0)
    grad_other = lax.ppermute(grad_own, "core", SWAP)

    out = jax.ShapeDtypeStruct((X, C, own, slice_width), BF16)
    partial = call(functools.partial(partial_kernel, 0), out, place, grad_own, head)
    partial = call(functools.partial(partial_kernel, 1), out, place, grad_other, head, partial, aliases={3: 0})
    over_x = lax.all_to_all(partial, "x", 0, 0)
    over_x, place, by_x, core, grad_own, grad_other = barrier((over_x, place, by_x, core, grad_own, grad_other))
    out = jax.ShapeDtypeStruct((Z, 2, hidden.size // 2), BF16)
    over_x = call(over_x_kernel, out, place, over_x)
    over_z = lax.all_to_all(over_x, "z", 0, 0)
    grad_hidden = jnp.sum(over_z.astype(F32), axis=0).astype(BF16).reshape(hidden.shape)

    def head_part(grad, half):
        rows = lax.dynamic_index_in_dim(by_x, half, 1, keepdims=False).reshape(-1, slice_width)
        grad = grad.reshape(-1, width)
        return lax.dot_general(grad, rows, (((0,), (0,)), ((), ())), preferred_element_type=F32)

    grad_head = (head_part(grad_own, core) + head_part(grad_other, 1 - core)).astype(BF16)
    return token_loss[0], grad_hidden, grad_head


def solution(mesh):
    torus = Mesh(mesh.devices.reshape(X, Z, Y, C), VOCAB_AXES + ROW_AXES)
    return jax.shard_map(
        per_device,
        mesh=torus,
        in_specs=(P(VOCAB_AXES, ROW_AXES), P(VOCAB_AXES, ROW_AXES), P(), P()),
        out_specs=(P(ROW_AXES), P(VOCAB_AXES, ROW_AXES), P(VOCAB_AXES, ROW_AXES)),
        check_vma=False,
    )
```

```python
import functools

import jax
import jax.numpy as jnp
from jax import lax
from jax.experimental import pallas as pl
from jax.experimental.pallas import tpu as pltpu
from jax.sharding import Mesh, PartitionSpec as P

X, Z, Y, C = 4, 16, 4, 2
VOCAB_AXES = ("x", "z")
ROW_AXES = ("y", "core")
SWAP = [(0, 1), (1, 0)]
LANES = 128
TILE = 256
BF16, F32 = jnp.bfloat16, jnp.float32
IN_VMEM = pl.BlockSpec(memory_space=pltpu.VMEM)
IN_SMEM = pl.BlockSpec(memory_space=pltpu.SMEM)


def call(kernel, out_shape, place, *operands, cost=None):
    many = isinstance(out_shape, list)
    moved = cost or sum(a.size * a.dtype.itemsize for a in operands)
    return pl.pallas_call(
        kernel,
        out_shape=out_shape,
        in_specs=[IN_SMEM] + [IN_VMEM] * len(operands),
        out_specs=[IN_VMEM] * len(out_shape) if many else IN_VMEM,
        cost_estimate=pl.CostEstimate(flops=moved, bytes_accessed=moved, transcendentals=0),
        compiler_params=pltpu.CompilerParams(vmem_limit_bytes=8 * 2**20),
    )(place, *operands)


def gather_over(block, axis):
    size = lax.axis_size(axis)
    copies = jnp.broadcast_to(block[None], (size,) + block.shape)
    return lax.all_to_all(copies, axis, 0, 0)


def to_lanes(column, first):
    shape = (column.shape[0], LANES)
    row, lane = (lax.broadcasted_iota(jnp.int32, shape, axis) for axis in (0, 1))
    return jnp.sum(jnp.where(row + first == lane, column, 0.0), axis=0, keepdims=True)


def to_column(lanes, rows, first=0):
    row, lane = (lax.broadcasted_iota(jnp.int32, (rows, LANES), axis) for axis in (0, 1))
    found = jnp.zeros((rows, LANES), lanes.dtype)
    for k in range(lanes.shape[0]):
        found = jnp.where(row + first == lane + k * LANES, lanes[k : k + 1], found)
    return jnp.sum(found, axis=1, keepdims=True)


def target_mask(place_ref, targets_ref, shape):
    column = to_column(targets_ref[...], shape[0], place_ref[1]) - place_ref[2]
    return lax.broadcasted_iota(jnp.int32, shape, 1) == column


def spans(length):
    return [pl.ds(first, min(TILE, length - first)) for first in range(0, length, TILE)]


def logits_kernel(place_ref, rows_ref, head_ref, other_ref, out_ref):
    mine = place_ref[0]
    own, rest = (
        rows_ref[:, pl.ds(c, 1)].reshape(-1, rows_ref.shape[-1]) for c in (mine, C - 1 - mine)
    )

    def dot(rows, part):
        return lax.dot_general(rows, part, (((1,), (1,)), ((), ())), preferred_element_type=F32)

    for span in spans(head_ref.shape[0]):
        tile = dot(own, head_ref[span, :]) + dot(rest, other_ref[span, :])
        out_ref[:, :, span] = tile.reshape(out_ref.shape[:2] + (span.size,))


def partial_kernel(place_ref, grad_ref, head_ref, other_ref, out_ref):
    mine = place_ref[0]
    blocks, _, own, slice_width = out_ref.shape
    grad = grad_ref[...].reshape(blocks * own, -1)
    for c, part_ref in ((mine, head_ref), (C - 1 - mine, other_ref)):
        for span in spans(slice_width):
            tile = jnp.dot(grad, part_ref[:, span], preferred_element_type=F32).astype(BF16)
            out_ref[:, pl.ds(c, 1), :, span] = tile.reshape(blocks, 1, own, span.size)


def statistics_kernel(place_ref, parts_ref, targets_ref, logits_ref, stats_ref):
    logits = parts_ref[0]
    for y in range(1, Y):
        logits = logits + parts_ref[y]
    logits_ref[...] = logits
    top = jnp.max(logits, axis=1, keepdims=True)
    total = jnp.sum(jnp.exp(logits - top), axis=1, keepdims=True)
    mask = target_mask(place_ref, targets_ref, logits.shape)
    target_logit = jnp.sum(jnp.where(mask, logits, 0.0), axis=1, keepdims=True)
    row = to_lanes(top + jnp.log(total), 0) + to_lanes(target_logit, LANES // 2)
    stats_ref[...] = jnp.broadcast_to(row[None], stats_ref.shape)


def softmax_kernel(place_ref, stats_ref, logits_ref, targets_ref, upstream_ref, loss_ref, grad_ref):
    logits = logits_ref[...]
    rows = logits.shape[0]
    stats = stats_ref[:, 0, :]
    top = jnp.max(stats, axis=0, keepdims=True)
    lse = to_column(top + jnp.log(jnp.sum(jnp.exp(stats - top), axis=0, keepdims=True)), rows)
    target_logit = to_column(jnp.sum(stats, axis=0, keepdims=True), rows, LANES // 2)
    loss_ref[...] = to_lanes(lse - target_logit, 0)[:, :rows]
    weight = to_column(upstream_ref[...], rows, place_ref[1])
    mask = target_mask(place_ref, targets_ref, logits.shape)
    probability = jnp.exp(logits - lse)
    grad = ((probability - jnp.where(mask, 1.0, 0.0)) * weight).astype(BF16)
    grad_ref[...] = jnp.broadcast_to(grad[None], grad_ref.shape)


def over_x_kernel(place_ref, parts_ref, out_ref):
    slice_width = parts_ref.shape[-1]
    blocks, pieces, _ = out_ref.shape
    block = out_ref.shape[2] // slice_width
    per_half = blocks // C
    for half in range(C):
        rows = parts_ref[0, half].astype(F32)
        for x in range(1, X):
            rows = rows + parts_ref[x, half].astype(F32)
        for k in range(per_half):
            for part in range(pieces):
                for row in range(block):
                    first = k * pieces * block + part * block + row
                    span = pl.ds(row * slice_width, slice_width)
                    out_ref[half * per_half + k, part : part + 1, span] = rows[first : first + 1].astype(BF16)


def head_kernel(place_ref, rows_ref, grad_ref, rest_rows_ref, rest_grad_ref, out_ref):
    mine = place_ref[0]
    width, slice_width = out_ref.shape
    rows = rows_ref[:, pl.ds(mine, 1)].reshape(-1, slice_width)
    rest_rows = rest_rows_ref[...].reshape(-1, slice_width)

    def dot(grad_ref, span, rows):
        grad = grad_ref[:, :, span].reshape(-1, span.size)
        return lax.dot_general(grad, rows, (((0,), (0,)), ((), ())), preferred_element_type=F32)

    for span in spans(width):
        out_ref[span, :] = (dot(grad_ref, span, rows) + dot(rest_grad_ref, span, rest_rows)).astype(BF16)


def per_device(hidden, head, targets, upstream):
    width, slice_width = head.shape
    token_count = targets.shape[0]
    own = token_count // (Y * C)
    barrier = lax.optimization_barrier

    core = lax.axis_index("core")
    row_first = lax.axis_index(ROW_AXES) * own
    first_column = lax.axis_index(VOCAB_AXES) * width
    hidden, core, row_first, first_column = barrier((hidden, core, row_first, first_column))
    by_z = gather_over(hidden.reshape(2, -1), "z").reshape(C, own, slice_width)

    by_z, head = barrier((by_z, head))
    head_other = lax.ppermute(head, "core", SWAP)
    copies = jnp.broadcast_to(by_z, (X, C, own, slice_width)).reshape(X * C, own, slice_width)
    by_x = lax.all_to_all(copies, ("x", "core"), 0, 0).reshape(X, C, own, slice_width)

    by_x, targets, upstream, core, row_first, first_column = barrier(
        (by_x, targets, upstream, core, row_first, first_column)
    )
    place = jnp.stack([core, row_first, first_column])
    targets, upstream = targets.reshape(-1, LANES), upstream.reshape(-1, LANES)
    out = jax.ShapeDtypeStruct((Y, own, width), F32)
    chip_logits = call(logits_kernel, out, place, by_x, head, head_other)
    chip_logits, targets, upstream = barrier((chip_logits, targets, upstream))
    parts = lax.all_to_all(chip_logits, "y", 0, 0)

    out = [jax.ShapeDtypeStruct((own, width), F32), jax.ShapeDtypeStruct((X * Z, 1, LANES), F32)]
    logits, stats = call(statistics_kernel, out, place, parts, targets)
    stats = lax.all_to_all(stats, VOCAB_AXES, 0, 0)
    out = [jax.ShapeDtypeStruct((1, own), F32), jax.ShapeDtypeStruct((Y, own, width), BF16)]
    token_loss, grad_rows = call(softmax_kernel, out, place, stats, logits, targets, upstream)

    grad_half = lax.all_to_all(grad_rows, "y", 0, 0)

    out = jax.ShapeDtypeStruct((X, C, own, slice_width), BF16)
    partial = call(partial_kernel, out, place, grad_half, head, head_other)
    over_x = lax.all_to_all(partial.reshape(X * C, own, slice_width), ("x", "core"), 0, 0).reshape(out.shape)
    out = jax.ShapeDtypeStruct((Z, 2, hidden.size // 2), BF16)
    over_x = call(over_x_kernel, out, place, over_x)
    over_x, by_x, core, grad_half, place = barrier((over_x, by_x, core, grad_half, place))
    over_z = lax.all_to_all(over_x, "z", 0, 0)
    grad_hidden = jnp.sum(over_z.astype(F32), axis=0).astype(BF16).reshape(hidden.shape)

    grad_rest = lax.ppermute(grad_half, "core", SWAP)
    rows_rest = lax.dynamic_index_in_dim(by_x, 1 - core, 1)
    rows_rest = lax.ppermute(rows_rest, "core", SWAP)
    out = jax.ShapeDtypeStruct((width, slice_width), BF16)
    grad_head = call(head_kernel, out, place, by_x, grad_half, rows_rest, grad_rest, cost=1)
    return token_loss[0], grad_hidden, grad_head


def solution(mesh):
    torus = Mesh(mesh.devices.reshape(X, Z, Y, C), VOCAB_AXES + ROW_AXES)
    return jax.shard_map(
        per_device,
        mesh=torus,
        in_specs=(P(VOCAB_AXES, ROW_AXES), P(VOCAB_AXES, ROW_AXES), P(), P()),
        out_specs=(P(ROW_AXES), P(VOCAB_AXES, ROW_AXES), P(VOCAB_AXES, ROW_AXES)),
        check_vma=False,
    )
```

```python
import functools

import jax
import jax.numpy as jnp
from jax import lax
from jax.experimental import pallas as pl
from jax.experimental.pallas import tpu as pltpu
from jax.sharding import Mesh, PartitionSpec as P

X, ZH, ZL, Y, C = 4, 8, 2, 4, 2
VOCAB_AXES = ("x", "zh", "zl")
NEAR_AXES = ("x", "zl", "core")
ROW_AXES = ("y", "core")
SWAP = [(0, 1), (1, 0)]
LANES = 128
PACK_COST = 2**26
TILE = 256
BF16, F32 = jnp.bfloat16, jnp.float32
IN_VMEM = pl.BlockSpec(memory_space=pltpu.VMEM)
IN_ANY = pl.BlockSpec(memory_space=pl.ANY)
IN_SMEM = pl.BlockSpec(memory_space=pltpu.SMEM)


def call(kernel, out_shape, place, *operands, cost=None, scratch=(), last=IN_VMEM):
    many = isinstance(out_shape, list)
    moved = cost or sum(a.size * a.dtype.itemsize for a in operands)
    return pl.pallas_call(
        kernel,
        out_shape=out_shape,
        in_specs=[IN_SMEM] + [IN_VMEM] * (len(operands) - 1) + [last],
        out_specs=[IN_VMEM] * len(out_shape) if many else IN_VMEM,
        scratch_shapes=scratch,
        cost_estimate=pl.CostEstimate(flops=moved, bytes_accessed=moved, transcendentals=0),
        compiler_params=pltpu.CompilerParams(vmem_limit_bytes=8 * 2**20),
    )(place, *operands)


def gather_over(block, axis):
    size = lax.axis_size(axis)
    copies = jnp.broadcast_to(block[None], (size,) + block.shape)
    return lax.all_to_all(copies, axis, 0, 0)


def to_lanes(column, position):
    lane = lax.broadcasted_iota(jnp.int32, (column.shape[0], LANES), 1)
    return jnp.sum(jnp.where(position == lane, column, 0.0), axis=0, keepdims=True)


def to_column(lanes, position):
    lane = lax.broadcasted_iota(jnp.int32, (position.shape[0], LANES), 1)
    found = jnp.zeros(lane.shape, lanes.dtype)
    for k in range(lanes.shape[0]):
        found = jnp.where(position == lane + k * LANES, lanes[k : k + 1], found)
    return jnp.sum(found, axis=1, keepdims=True)


def row_iota(rows):
    return lax.broadcasted_iota(jnp.int32, (rows, 1), 0)


def token_position(rows):
    block = rows * C // (ZH * ZL)
    row = row_iota(rows)
    zl, rest = row // (rows // ZL), row % (rows // ZL)
    return rest // block * (ZL * block) + zl * block + rest % block


def target_mask(place_ref, targets_ref, shape):
    column = to_column(targets_ref[...], token_position(shape[0]) + place_ref[1]) - place_ref[2]
    return lax.broadcasted_iota(jnp.int32, shape, 1) == column


def spans(length):
    return [pl.ds(first, min(TILE, length - first)) for first in range(0, length, TILE)]


def logits_kernel(place_ref, rows_ref, head_ref, other_ref, out_ref, kept_ref, sem):
    keep = pltpu.make_async_copy(other_ref, kept_ref, sem)
    keep.start()
    mine = place_ref[0]

    def tile(c, part_ref, span):
        rows = rows_ref[:, :, pl.ds(c, 1)].reshape(-1, rows_ref.shape[-1])
        product = lax.dot_general(rows, part_ref[span, :], (((1,), (1,)), ((), ())), preferred_element_type=F32)
        return product.reshape(out_ref.shape[:2] + (span.size,))

    for span in spans(head_ref.shape[0]):
        out_ref[:, :, span] = tile(mine, head_ref, span)
    keep.wait()
    for span in spans(head_ref.shape[0]):
        out_ref[:, :, span] += tile(C - 1 - mine, kept_ref, span)


def partial_kernel(place_ref, grad_ref, head_ref, other_ref, out_ref):
    mine = place_ref[0]
    _, _, _, rows, slice_width = out_ref.shape
    grad = grad_ref[...].reshape(X * ZL * rows, -1)
    for c, part_ref in ((mine, head_ref), (C - 1 - mine, other_ref)):
        for span in spans(slice_width):
            tile = jnp.dot(grad, part_ref[:, span], preferred_element_type=F32).astype(BF16)
            out_ref[:, :, pl.ds(c, 1), :, span] = tile.reshape(X, ZL, 1, rows, span.size)


def statistics_kernel(place_ref, parts_ref, targets_ref, logits_ref, stats_ref):
    logits = parts_ref[0]
    for y in range(1, Y):
        logits = logits + parts_ref[y]
    logits_ref[...] = logits
    top = jnp.max(logits, axis=1, keepdims=True)
    total = jnp.sum(jnp.exp(logits - top), axis=1, keepdims=True)
    mask = target_mask(place_ref, targets_ref, logits.shape)
    target_logit = jnp.sum(jnp.where(mask, logits, 0.0), axis=1, keepdims=True)
    row = row_iota(logits.shape[0])
    row = to_lanes(top + jnp.log(total), row) + to_lanes(target_logit, row + LANES // 2)
    stats_ref[...] = jnp.broadcast_to(row[None], stats_ref.shape)


def softmax_kernel(place_ref, stats_ref, logits_ref, targets_ref, upstream_ref, loss_ref, grad_ref):
    logits = logits_ref[...]
    rows = logits.shape[0]
    stats = stats_ref[:, 0, :]
    top = jnp.max(stats, axis=0, keepdims=True)
    row = row_iota(rows)
    lse = to_column(top + jnp.log(jnp.sum(jnp.exp(stats - top), axis=0, keepdims=True)), row)
    target_logit = to_column(jnp.sum(stats, axis=0, keepdims=True), row + LANES // 2)
    position = token_position(rows)
    loss_ref[...] = to_lanes(lse - target_logit, position)[:, :rows]
    weight = to_column(upstream_ref[...], position + place_ref[1])
    mask = target_mask(place_ref, targets_ref, logits.shape)
    probability = jnp.exp(logits - lse)
    grad = ((probability - jnp.where(mask, 1.0, 0.0)) * weight).astype(BF16)
    grad_ref[...] = jnp.broadcast_to(grad[None], grad_ref.shape)


def over_x_kernel(place_ref, parts_ref, out_ref):
    blocks, pieces, rows, _ = out_ref.shape
    per_half = blocks // C
    for half in range(C):
        total = 0.0
        for x in range(X):
            for zl in range(ZL):
                total = total + parts_ref[x, zl, half].astype(F32)
        for k in range(per_half * pieces):
            piece = total[k * rows : (k + 1) * rows].astype(BF16)
            out_ref[half * per_half + k // pieces, k % pieces] = piece


def pack_kernel(place_ref, rows_ref, grad_ref, out_ref):
    width, slice_width = grad_ref.shape[-1], rows_ref.shape[-1]
    out_ref[:, :, :width] = grad_ref[...]
    rows = rows_ref[:, :, pl.ds(C - 1 - place_ref[0], 1)]
    out_ref[:, :, out_ref.shape[-1] - slice_width :] = rows.reshape(Y, -1, slice_width)


def pick_kernel(place_ref, rows_ref, out_ref):
    out_ref[...] = rows_ref[:, :, pl.ds(place_ref[0], 1)].reshape(out_ref.shape)


def head_kernel(place_ref, rows_ref, grad_ref, rest_ref, out_ref):
    width, slice_width = out_ref.shape
    rows = rows_ref[...]
    rest_rows = rest_ref[:, :, rest_ref.shape[-1] - slice_width :].reshape(-1, slice_width)

    def dot(grad_ref, span, rows):
        grad = grad_ref[:, :, span].reshape(-1, span.size)
        return lax.dot_general(grad, rows, (((0,), (0,)), ((), ())), preferred_element_type=F32)

    for span in spans(width):
        out_ref[span, :] = (dot(grad_ref, span, rows) + dot(rest_ref, span, rest_rows)).astype(BF16)


def per_device(hidden, head, targets, upstream):
    width, slice_width = head.shape
    token_count = targets.shape[0]
    own = token_count // (Y * C)
    near = (X, ZL, C, own // ZL, slice_width)
    barrier = lax.optimization_barrier

    core = lax.axis_index("core")
    row_first = lax.axis_index(ROW_AXES) * own
    first_column = lax.axis_index(VOCAB_AXES) * width
    hidden, core, row_first, first_column = barrier((hidden, core, row_first, first_column))
    by_z = gather_over(hidden.reshape(-1, 2, slice_width), "zh").reshape(near[2:])

    by_z, head = barrier((by_z, head))
    head_other = lax.ppermute(head, "core", SWAP)
    copies = jnp.broadcast_to(by_z, near).reshape(-1, *near[3:])
    by_x = lax.all_to_all(copies, NEAR_AXES, 0, 0).reshape(near)

    by_x, targets, upstream, core, row_first, first_column = barrier(
        (by_x, targets, upstream, core, row_first, first_column)
    )
    place = jnp.stack([core, row_first, first_column])
    targets, upstream = targets.reshape(-1, LANES), upstream.reshape(-1, LANES)
    out = [jax.ShapeDtypeStruct((Y, own, width), F32), jax.ShapeDtypeStruct(head.shape, BF16)]
    sem = [pltpu.SemaphoreType.DMA]
    chip_logits, head_other = call(logits_kernel, out, place, by_x, head, head_other, scratch=sem, last=IN_ANY)
    chip_logits, targets, upstream = barrier((chip_logits, targets, upstream))
    parts = lax.all_to_all(chip_logits, "y", 0, 0)

    out = [jax.ShapeDtypeStruct((own, width), F32), jax.ShapeDtypeStruct((X * ZH * ZL, 1, LANES), F32)]
    logits, stats = call(statistics_kernel, out, place, parts, targets)
    stats = lax.all_to_all(stats, VOCAB_AXES, 0, 0)
    out = [jax.ShapeDtypeStruct((1, own), F32), jax.ShapeDtypeStruct((Y, own, width), BF16)]
    token_loss, grad_rows = call(softmax_kernel, out, place, stats, logits, targets, upstream)

    grad_half = lax.all_to_all(grad_rows, "y", 0, 0)

    partial = call(partial_kernel, jax.ShapeDtypeStruct(near, BF16), place, grad_half, head, head_other)
    padded = -(-width // LANES) * LANES
    out = jax.ShapeDtypeStruct((Y, own, padded + slice_width), BF16)
    rest = call(pack_kernel, out, place, by_x, grad_half, cost=PACK_COST)
    rest = lax.ppermute(rest, "core", SWAP)
    over_x = lax.all_to_all(partial.reshape(-1, *near[3:]), NEAR_AXES, 0, 0).reshape(near)
    out = jax.ShapeDtypeStruct((ZH, hidden.shape[0] // 2, 2, slice_width), BF16)
    over_x = call(over_x_kernel, out, place, over_x)
    over_x, by_x, core, grad_half, place = barrier((over_x, by_x, core, grad_half, place))
    over_z = lax.all_to_all(over_x, "zh", 0, 0)

    out = jax.ShapeDtypeStruct((Y * own, slice_width), BF16)
    rows = call(pick_kernel, out, place, by_x, cost=PACK_COST)
    out = jax.ShapeDtypeStruct((width, slice_width), BF16)
    grad_head = call(head_kernel, out, place, rows, grad_half, rest, cost=1)
    over_z, grad_head = barrier((over_z, grad_head))
    grad_hidden = jnp.sum(over_z.astype(F32), axis=0).astype(BF16).reshape(hidden.shape)
    return token_loss[0], grad_hidden, grad_head


def solution(mesh):
    torus = Mesh(mesh.devices.reshape(X, ZH, ZL, Y, C), VOCAB_AXES + ROW_AXES)
    return jax.shard_map(
        per_device,
        mesh=torus,
        in_specs=(P(VOCAB_AXES, ROW_AXES), P(VOCAB_AXES, ROW_AXES), P(), P()),
        out_specs=(P(ROW_AXES), P(VOCAB_AXES, ROW_AXES), P(VOCAB_AXES, ROW_AXES)),
        check_vma=False,
    )
```

```python
import functools

import jax
import jax.numpy as jnp
from jax import lax
from jax.experimental import pallas as pl
from jax.experimental.pallas import tpu as pltpu
from jax.sharding import Mesh, PartitionSpec as P

X, ZH, ZL, Y, C = 4, 8, 2, 4, 2
VOCAB_AXES = ("x", "zh", "zl")
NEAR_AXES = ("x", "zl", "core")
ROW_AXES = ("y", "core")
SWAP = [(0, 1), (1, 0)]
LANES = 128
PACK_COST = 2**26
TILE = 256
BF16, F32 = jnp.bfloat16, jnp.float32
IN_VMEM = pl.BlockSpec(memory_space=pltpu.VMEM)
IN_ANY = pl.BlockSpec(memory_space=pl.ANY)
IN_SMEM = pl.BlockSpec(memory_space=pltpu.SMEM)


def call(kernel, out_shape, place, *operands, cost=None, scratch=(), last=IN_VMEM, result=IN_VMEM, aliases=None):
    many = isinstance(out_shape, list)
    moved = cost or sum(a.size * a.dtype.itemsize for a in operands)
    return pl.pallas_call(
        kernel,
        out_shape=out_shape,
        in_specs=[IN_SMEM] + [IN_VMEM] * (len(operands) - 1) + [last],
        out_specs=[IN_VMEM] * len(out_shape) if many else result,
        scratch_shapes=scratch,
        input_output_aliases=aliases or {},
        cost_estimate=pl.CostEstimate(flops=moved, bytes_accessed=moved, transcendentals=0),
        compiler_params=pltpu.CompilerParams(vmem_limit_bytes=8 * 2**20),
    )(place, *operands)


def gather_over(block, axis):
    size = lax.axis_size(axis)
    copies = jnp.broadcast_to(block[None], (size,) + block.shape)
    return lax.all_to_all(copies, axis, 0, 0)


def to_lanes(column, position):
    lane = lax.broadcasted_iota(jnp.int32, (column.shape[0], LANES), 1)
    return jnp.sum(jnp.where(position == lane, column, 0.0), axis=0, keepdims=True)


def to_column(lanes, position):
    lane = lax.broadcasted_iota(jnp.int32, (position.shape[0], LANES), 1)
    found = jnp.zeros(lane.shape, lanes.dtype)
    for k in range(lanes.shape[0]):
        found = jnp.where(position == lane + k * LANES, lanes[k : k + 1], found)
    return jnp.sum(found, axis=1, keepdims=True)


def row_iota(rows):
    return lax.broadcasted_iota(jnp.int32, (rows, 1), 0)


def token_position(rows):
    block = rows * C // (ZH * ZL)
    row = row_iota(rows)
    zl, rest = row // (rows // ZL), row % (rows // ZL)
    return rest // block * (ZL * block) + zl * block + rest % block


def target_mask(place_ref, targets_ref, shape):
    column = to_column(targets_ref[...], token_position(shape[0]) + place_ref[1]) - place_ref[2]
    return lax.broadcasted_iota(jnp.int32, shape, 1) == column


def spans(length):
    return [pl.ds(first, min(TILE, length - first)) for first in range(0, length, TILE)]


def logits_kernel(place_ref, rows_ref, head_ref, other_ref, out_ref, kept_ref, sem):
    keep = pltpu.make_async_copy(other_ref, kept_ref, sem)
    keep.start()
    mine = place_ref[0]

    def tile(c, part_ref, span):
        rows = rows_ref[:, :, pl.ds(c, 1)].reshape(-1, rows_ref.shape[-1])
        product = lax.dot_general(rows, part_ref[span, :], (((1,), (1,)), ((), ())), preferred_element_type=F32)
        return product.reshape(out_ref.shape[:2] + (span.size,))

    for span in spans(head_ref.shape[0]):
        out_ref[:, :, span] = tile(mine, head_ref, span)
    keep.wait()
    for span in spans(head_ref.shape[0]):
        out_ref[:, :, span] += tile(C - 1 - mine, kept_ref, span)


def partial_kernel(place_ref, grad_ref, head_ref, other_ref, spent_ref, out_ref, held_ref, sems):
    mine = place_ref[0]
    _, _, _, rows, slice_width = out_ref.shape
    grad = grad_ref[...].reshape(X * ZL * rows, -1)
    copies = []
    for k, (c, part_ref) in enumerate(((mine, head_ref), (C - 1 - mine, other_ref))):
        for span in spans(slice_width):
            tile = jnp.dot(grad, part_ref[:, span], preferred_element_type=F32).astype(BF16)
            held_ref[k, :, :, :, span] = tile.reshape(X, ZL, rows, span.size)
        copies.append(pltpu.make_async_copy(held_ref.at[k], out_ref.at[:, :, c], sems.at[k]))
        copies[-1].start()
    for copy in copies:
        copy.wait()


def statistics_kernel(place_ref, parts_ref, targets_ref, logits_ref, stats_ref):
    logits = parts_ref[0]
    for y in range(1, Y):
        logits = logits + parts_ref[y]
    logits_ref[...] = logits
    top = jnp.max(logits, axis=1, keepdims=True)
    total = jnp.sum(jnp.exp(logits - top), axis=1, keepdims=True)
    mask = target_mask(place_ref, targets_ref, logits.shape)
    target_logit = jnp.sum(jnp.where(mask, logits, 0.0), axis=1, keepdims=True)
    row = row_iota(logits.shape[0])
    row = to_lanes(top + jnp.log(total), row) + to_lanes(target_logit, row + LANES // 2)
    stats_ref[...] = jnp.broadcast_to(row[None], stats_ref.shape)


def softmax_kernel(place_ref, stats_ref, logits_ref, targets_ref, upstream_ref, loss_ref, grad_ref):
    logits = logits_ref[...]
    rows = logits.shape[0]
    stats = stats_ref[:, 0, :]
    top = jnp.max(stats, axis=0, keepdims=True)
    row = row_iota(rows)
    lse = to_column(top + jnp.log(jnp.sum(jnp.exp(stats - top), axis=0, keepdims=True)), row)
    target_logit = to_column(jnp.sum(stats, axis=0, keepdims=True), row + LANES // 2)
    position = token_position(rows)
    loss_ref[...] = to_lanes(lse - target_logit, position)[:, :rows]
    weight = to_column(upstream_ref[...], position + place_ref[1])
    mask = target_mask(place_ref, targets_ref, logits.shape)
    probability = jnp.exp(logits - lse)
    grad = ((probability - jnp.where(mask, 1.0, 0.0)) * weight).astype(BF16)
    grad_ref[...] = jnp.broadcast_to(grad[None], grad_ref.shape)


def over_x_kernel(place_ref, parts_ref, out_ref):
    blocks, pieces, rows, _ = out_ref.shape
    per_half = blocks // C
    for half in range(C):
        total = 0.0
        for x in range(X):
            for zl in range(ZL):
                total = total + parts_ref[x, zl, half].astype(F32)
        for k in range(per_half * pieces):
            piece = total[k * rows : (k + 1) * rows].astype(BF16)
            out_ref[half * per_half + k // pieces, k % pieces] = piece


def pack_kernel(place_ref, rows_ref, grad_ref, out_ref):
    width, slice_width = grad_ref.shape[-1], rows_ref.shape[-1]
    out_ref[:, :, :width] = grad_ref[...]
    rows = rows_ref[:, :, pl.ds(C - 1 - place_ref[0], 1)]
    out_ref[:, :, out_ref.shape[-1] - slice_width :] = rows.reshape(Y, -1, slice_width)


def pick_kernel(place_ref, rows_ref, out_ref):
    out_ref[...] = rows_ref[:, :, pl.ds(place_ref[0], 1)].reshape(out_ref.shape)


def head_kernel(place_ref, rows_ref, grad_ref, rest_ref, out_ref):
    width, slice_width = out_ref.shape
    rows = rows_ref[...]
    rest_rows = rest_ref[:, :, rest_ref.shape[-1] - slice_width :].reshape(-1, slice_width)

    def dot(grad_ref, span, rows):
        grad = grad_ref[:, :, span].reshape(-1, span.size)
        return lax.dot_general(grad, rows, (((0,), (0,)), ((), ())), preferred_element_type=F32)

    for span in spans(width):
        out_ref[span, :] = (dot(grad_ref, span, rows) + dot(rest_ref, span, rest_rows)).astype(BF16)


def per_device(hidden, head, targets, upstream):
    width, slice_width = head.shape
    token_count = targets.shape[0]
    own = token_count // (Y * C)
    near = (X, ZL, C, own // ZL, slice_width)
    barrier = lax.optimization_barrier

    core = lax.axis_index("core")
    row_first = lax.axis_index(ROW_AXES) * own
    first_column = lax.axis_index(VOCAB_AXES) * width
    hidden, core, row_first, first_column = barrier((hidden, core, row_first, first_column))
    by_z = gather_over(hidden.reshape(-1, 2, slice_width), "zh").reshape(near[2:])

    by_z, head = barrier((by_z, head))
    head_other = lax.ppermute(head, "core", SWAP)
    copies = jnp.broadcast_to(by_z, near).reshape(-1, *near[3:])
    by_x = lax.all_to_all(copies, NEAR_AXES, 0, 0).reshape(near)

    by_x, targets, upstream, core, row_first, first_column = barrier(
        (by_x, targets, upstream, core, row_first, first_column)
    )
    place = jnp.stack([core, row_first, first_column])
    targets, upstream = targets.reshape(-1, LANES), upstream.reshape(-1, LANES)
    out = [jax.ShapeDtypeStruct((Y, own, width), F32), jax.ShapeDtypeStruct(head.shape, BF16)]
    sem = [pltpu.SemaphoreType.DMA]
    chip_logits, head_other = call(logits_kernel, out, place, by_x, head, head_other, scratch=sem, last=IN_ANY)
    chip_logits, targets, upstream = barrier((chip_logits, targets, upstream))
    parts = lax.all_to_all(chip_logits, "y", 0, 0)

    out = [jax.ShapeDtypeStruct((own, width), F32), jax.ShapeDtypeStruct((X * ZH * ZL, 1, LANES), F32)]
    logits, stats = call(statistics_kernel, out, place, parts, targets)
    stats = lax.all_to_all(stats, VOCAB_AXES, 0, 0)
    out = [jax.ShapeDtypeStruct((1, own), F32), jax.ShapeDtypeStruct((Y, own, width), BF16)]
    token_loss, grad_rows = call(softmax_kernel, out, place, stats, logits, targets, upstream)

    grad_half = lax.all_to_all(grad_rows, "y", 0, 0)

    held = [pltpu.VMEM((C, X, ZL, *near[3:]), BF16), pltpu.SemaphoreType.DMA((C,))]
    out = jax.ShapeDtypeStruct(near, BF16)
    partial = call(
        partial_kernel, out, place, grad_half, head, head_other, copies.reshape(near),
        scratch=held, last=IN_ANY, result=IN_ANY, aliases={4: 0},
    )
    padded = -(-width // LANES) * LANES
    out = jax.ShapeDtypeStruct((Y, own, padded + slice_width), BF16)
    rest = call(pack_kernel, out, place, by_x, grad_half, cost=PACK_COST)
    rest = lax.ppermute(rest, "core", SWAP)
    over_x = lax.all_to_all(partial.reshape(-1, *near[3:]), NEAR_AXES, 0, 0).reshape(near)
    out = jax.ShapeDtypeStruct((ZH, hidden.shape[0] // 2, 2, slice_width), BF16)
    over_x = call(over_x_kernel, out, place, over_x)
    over_x, by_x, core, grad_half, place = barrier((over_x, by_x, core, grad_half, place))
    over_z = lax.all_to_all(over_x, "zh", 0, 0)

    out = jax.ShapeDtypeStruct((Y * own, slice_width), BF16)
    rows = call(pick_kernel, out, place, by_x, cost=PACK_COST)
    out = jax.ShapeDtypeStruct((width, slice_width), BF16)
    grad_head = call(head_kernel, out, place, rows, grad_half, rest, cost=1)
    over_z, grad_head = barrier((over_z, grad_head))
    grad_hidden = jnp.sum(over_z.astype(F32), axis=0).astype(BF16).reshape(hidden.shape)
    return token_loss[0], grad_hidden, grad_head


def solution(mesh):
    torus = Mesh(mesh.devices.reshape(X, ZH, ZL, Y, C), VOCAB_AXES + ROW_AXES)
    return jax.shard_map(
        per_device,
        mesh=torus,
        in_specs=(P(VOCAB_AXES, ROW_AXES), P(VOCAB_AXES, ROW_AXES), P(), P()),
        out_specs=(P(ROW_AXES), P(VOCAB_AXES, ROW_AXES), P(VOCAB_AXES, ROW_AXES)),
        check_vma=False,
    )
```

```python
import functools

import jax
import jax.numpy as jnp
from jax import lax
from jax.experimental import pallas as pl
from jax.experimental.pallas import tpu as pltpu
from jax.sharding import Mesh, PartitionSpec as P

X, ZH, ZL, Y, C = 4, 8, 2, 4, 2
VOCAB_AXES = ("x", "zh", "zl")
NEAR_AXES = ("x", "zl", "core")
ROW_AXES = ("y", "core")
SWAP = [(0, 1), (1, 0)]
LANES = 128
PACK_COST = 2**26
TILE = 256
BF16, F32 = jnp.bfloat16, jnp.float32
IN_VMEM = pl.BlockSpec(memory_space=pltpu.VMEM)
IN_ANY = pl.BlockSpec(memory_space=pl.ANY)
IN_SMEM = pl.BlockSpec(memory_space=pltpu.SMEM)


def call(kernel, out_shape, place, *operands, cost=None, scratch=(), last=IN_VMEM, result=IN_VMEM, aliases=None):
    many = isinstance(out_shape, list)
    moved = cost or sum(a.size * a.dtype.itemsize for a in operands)
    return pl.pallas_call(
        kernel,
        out_shape=out_shape,
        in_specs=[IN_SMEM] + [IN_VMEM] * (len(operands) - 1) + [last],
        out_specs=[IN_VMEM] * len(out_shape) if many else result,
        scratch_shapes=scratch,
        input_output_aliases=aliases or {},
        cost_estimate=pl.CostEstimate(flops=moved, bytes_accessed=moved, transcendentals=0),
        compiler_params=pltpu.CompilerParams(vmem_limit_bytes=8 * 2**20),
    )(place, *operands)


def gather_over(block, axis):
    size = lax.axis_size(axis)
    copies = jnp.broadcast_to(block[None], (size,) + block.shape)
    return lax.all_to_all(copies, axis, 0, 0)


def to_lanes(column, position):
    lane = lax.broadcasted_iota(jnp.int32, (column.shape[0], LANES), 1)
    return jnp.sum(jnp.where(position == lane, column, 0.0), axis=0, keepdims=True)


def to_column(lanes, position):
    lane = lax.broadcasted_iota(jnp.int32, (position.shape[0], LANES), 1)
    found = jnp.zeros(lane.shape, lanes.dtype)
    for k in range(lanes.shape[0]):
        found = jnp.where(position == lane + k * LANES, lanes[k : k + 1], found)
    return jnp.sum(found, axis=1, keepdims=True)


def row_iota(rows):
    return lax.broadcasted_iota(jnp.int32, (rows, 1), 0)


def token_position(rows):
    block = rows * C // (ZH * ZL)
    row = row_iota(rows)
    zl, rest = row // (rows // ZL), row % (rows // ZL)
    return rest // block * (ZL * block) + zl * block + rest % block


def target_mask(place_ref, targets_ref, shape):
    column = to_column(targets_ref[...], token_position(shape[0]) + place_ref[1]) - place_ref[2]
    return lax.broadcasted_iota(jnp.int32, shape, 1) == column


def spans(length):
    return [pl.ds(first, min(TILE, length - first)) for first in range(0, length, TILE)]


def logits_kernel(place_ref, rows_ref, head_ref, other_ref, out_ref, kept_ref, sem):
    keep = pltpu.make_async_copy(other_ref, kept_ref, sem)
    keep.start()
    mine = place_ref[0]

    width = head_ref.shape[0]

    def tile(c, part_ref, span):
        rows = rows_ref[:, :, pl.ds(c, 1)].reshape(-1, rows_ref.shape[-1])
        product = lax.dot_general(rows, part_ref[span, :], (((1,), (1,)), ((), ())), preferred_element_type=F32)
        return product.reshape(Y, ZL, -1, span.size)

    for span in spans(width):
        product = tile(mine, head_ref, span)
        for zl in range(ZL):
            out_ref[:, :, pl.ds(zl * width + span.start, span.size)] = product[:, zl]
    keep.wait()
    for span in spans(width):
        product = tile(C - 1 - mine, kept_ref, span)
        for zl in range(ZL):
            out_ref[:, :, pl.ds(zl * width + span.start, span.size)] += product[:, zl]


def partial_kernel(place_ref, grad_ref, head_ref, other_ref, spent_ref, out_ref, held_ref, sems):
    mine = place_ref[0]
    _, _, _, rows, slice_width = out_ref.shape
    grad = grad_ref[...].reshape(X * ZL * rows, -1)
    copies = []
    for k, (c, part_ref) in enumerate(((mine, head_ref), (C - 1 - mine, other_ref))):
        for span in spans(slice_width):
            tile = jnp.dot(grad, part_ref[:, span], preferred_element_type=F32).astype(BF16)
            held_ref[k, :, :, :, span] = tile.reshape(X, ZL, rows, span.size)
        copies.append(pltpu.make_async_copy(held_ref.at[k], out_ref.at[:, :, c], sems.at[k]))
        copies[-1].start()
    for copy in copies:
        copy.wait()


def statistics_kernel(place_ref, parts_ref, targets_ref, logits_ref, stats_ref):
    logits = parts_ref[0]
    for y in range(1, Y):
        logits = logits + parts_ref[y]
    width = logits_ref.shape[1]
    logits = jnp.concatenate([logits[:, zl * width : (zl + 1) * width] for zl in range(ZL)], axis=0)
    logits_ref[...] = logits
    top = jnp.max(logits, axis=1, keepdims=True)
    total = jnp.sum(jnp.exp(logits - top), axis=1, keepdims=True)
    mask = target_mask(place_ref, targets_ref, logits.shape)
    target_logit = jnp.sum(jnp.where(mask, logits, 0.0), axis=1, keepdims=True)
    row = row_iota(logits.shape[0])
    row = to_lanes(top + jnp.log(total), row) + to_lanes(target_logit, row + LANES // 2)
    stats_ref[...] = jnp.broadcast_to(row[None], stats_ref.shape)


def softmax_kernel(place_ref, stats_ref, logits_ref, targets_ref, upstream_ref, loss_ref, grad_ref):
    logits = logits_ref[...]
    rows = logits.shape[0]
    stats = stats_ref[:, 0, :]
    top = jnp.max(stats, axis=0, keepdims=True)
    row = row_iota(rows)
    lse = to_column(top + jnp.log(jnp.sum(jnp.exp(stats - top), axis=0, keepdims=True)), row)
    target_logit = to_column(jnp.sum(stats, axis=0, keepdims=True), row + LANES // 2)
    position = token_position(rows)
    loss_ref[...] = to_lanes(lse - target_logit, position)[:, :rows]
    weight = to_column(upstream_ref[...], position + place_ref[1])
    mask = target_mask(place_ref, targets_ref, logits.shape)
    probability = jnp.exp(logits - lse)
    grad = ((probability - jnp.where(mask, 1.0, 0.0)) * weight).astype(BF16)
    grad_ref[...] = jnp.broadcast_to(grad[None], grad_ref.shape)


def over_x_kernel(place_ref, parts_ref, out_ref):
    blocks, pieces, rows, _ = out_ref.shape
    per_half = blocks // C
    for half in range(C):
        total = 0.0
        for x in range(X):
            for zl in range(ZL):
                total = total + parts_ref[x, zl, half].astype(F32)
        for k in range(per_half * pieces):
            piece = total[k * rows : (k + 1) * rows].astype(BF16)
            out_ref[half * per_half + k // pieces, k % pieces] = piece


def pack_kernel(place_ref, rows_ref, grad_ref, out_ref):
    width, slice_width = grad_ref.shape[-1], rows_ref.shape[-1]
    out_ref[:, :, :width] = grad_ref[...]
    rows = rows_ref[:, :, pl.ds(C - 1 - place_ref[0], 1)]
    out_ref[:, :, out_ref.shape[-1] - slice_width :] = rows.reshape(Y, -1, slice_width)


def pick_kernel(place_ref, rows_ref, out_ref):
    out_ref[...] = rows_ref[:, :, pl.ds(place_ref[0], 1)].reshape(out_ref.shape)


def head_kernel(place_ref, rows_ref, grad_ref, rest_ref, out_ref):
    width, slice_width = out_ref.shape
    rows = rows_ref[...]
    rest_rows = rest_ref[:, :, rest_ref.shape[-1] - slice_width :].reshape(-1, slice_width)

    def dot(grad_ref, span, rows):
        grad = grad_ref[:, :, span].reshape(-1, span.size)
        return lax.dot_general(grad, rows, (((0,), (0,)), ((), ())), preferred_element_type=F32)

    for span in spans(width):
        out_ref[span, :] = (dot(grad_ref, span, rows) + dot(rest_ref, span, rest_rows)).astype(BF16)


def per_device(hidden, head, targets, upstream):
    width, slice_width = head.shape
    token_count = targets.shape[0]
    own = token_count // (Y * C)
    near = (X, ZL, C, own // ZL, slice_width)
    barrier = lax.optimization_barrier

    core = lax.axis_index("core")
    row_first = lax.axis_index(ROW_AXES) * own
    first_column = lax.axis_index(VOCAB_AXES) * width
    hidden, core, row_first, first_column = barrier((hidden, core, row_first, first_column))
    by_z = gather_over(hidden.reshape(-1, 2, slice_width), "zh").reshape(near[2:])

    by_z, head = barrier((by_z, head))
    head_other = lax.ppermute(head, "core", SWAP)
    copies = jnp.broadcast_to(by_z, near).reshape(-1, *near[3:])
    by_x = lax.all_to_all(copies, NEAR_AXES, 0, 0).reshape(near)

    by_x, targets, upstream, core, row_first, first_column = barrier(
        (by_x, targets, upstream, core, row_first, first_column)
    )
    place = jnp.stack([core, row_first, first_column])
    targets, upstream = targets.reshape(-1, LANES), upstream.reshape(-1, LANES)
    out = [jax.ShapeDtypeStruct((Y, own // ZL, ZL * width), F32), jax.ShapeDtypeStruct(head.shape, BF16)]
    sem = [pltpu.SemaphoreType.DMA]
    chip_logits, head_other = call(logits_kernel, out, place, by_x, head, head_other, scratch=sem, last=IN_ANY)
    chip_logits, targets, upstream = barrier((chip_logits, targets, upstream))
    parts = lax.all_to_all(chip_logits, "y", 0, 0)

    out = [jax.ShapeDtypeStruct((own, width), F32), jax.ShapeDtypeStruct((X * ZH * ZL, 1, LANES), F32)]
    logits, stats = call(statistics_kernel, out, place, parts, targets)
    stats = lax.all_to_all(stats, VOCAB_AXES, 0, 0)
    out = [jax.ShapeDtypeStruct((1, own), F32), jax.ShapeDtypeStruct((Y, own, width), BF16)]
    token_loss, grad_rows = call(softmax_kernel, out, place, stats, logits, targets, upstream)

    grad_half = lax.all_to_all(grad_rows, "y", 0, 0)

    held = [pltpu.VMEM((C, X, ZL, *near[3:]), BF16), pltpu.SemaphoreType.DMA((C,))]
    out = jax.ShapeDtypeStruct(near, BF16)
    partial = call(
        partial_kernel, out, place, grad_half, head, head_other, copies.reshape(near),
        scratch=held, last=IN_ANY, result=IN_ANY, aliases={4: 0},
    )
    padded = -(-width // LANES) * LANES
    out = jax.ShapeDtypeStruct((Y, own, padded + slice_width), BF16)
    rest = call(pack_kernel, out, place, by_x, grad_half, cost=PACK_COST)
    rest = lax.ppermute(rest, "core", SWAP)
    over_x = lax.all_to_all(partial.reshape(-1, *near[3:]), NEAR_AXES, 0, 0).reshape(near)
    out = jax.ShapeDtypeStruct((ZH, hidden.shape[0] // 2, 2, slice_width), BF16)
    over_x = call(over_x_kernel, out, place, over_x)
    over_x, by_x, core, grad_half, place = barrier((over_x, by_x, core, grad_half, place))
    over_z = lax.all_to_all(over_x, "zh", 0, 0)

    out = jax.ShapeDtypeStruct((Y * own, slice_width), BF16)
    rows = call(pick_kernel, out, place, by_x, cost=PACK_COST)
    out = jax.ShapeDtypeStruct((width, slice_width), BF16)
    grad_head = call(head_kernel, out, place, rows, grad_half, rest, cost=1)
    over_z, grad_head = barrier((over_z, grad_head))
    grad_hidden = jnp.sum(over_z.astype(F32), axis=0).astype(BF16).reshape(hidden.shape)
    return token_loss[0], grad_hidden, grad_head


def solution(mesh):
    torus = Mesh(mesh.devices.reshape(X, ZH, ZL, Y, C), VOCAB_AXES + ROW_AXES)
    return jax.shard_map(
        per_device,
        mesh=torus,
        in_specs=(P(VOCAB_AXES, ROW_AXES), P(VOCAB_AXES, ROW_AXES), P(), P()),
        out_specs=(P(ROW_AXES), P(VOCAB_AXES, ROW_AXES), P(VOCAB_AXES, ROW_AXES)),
        check_vma=False,
    )
```

```python
import functools

import jax
import jax.numpy as jnp
from jax import lax
from jax.experimental import pallas as pl
from jax.experimental.pallas import tpu as pltpu
from jax.sharding import Mesh, PartitionSpec as P

X, ZH, ZL, Y, C = 4, 8, 2, 4, 2
VOCAB_AXES = ("x", "zh", "zl")
NEAR_AXES = ("x", "zl", "core")
ROW_AXES = ("y", "core")
SWAP = [(0, 1), (1, 0)]
LANES = 128
SUBLANES = 8
PACK_COST = 2**26
TILE = 256
BF16, F32 = jnp.bfloat16, jnp.float32
IN_VMEM = pl.BlockSpec(memory_space=pltpu.VMEM)
IN_ANY = pl.BlockSpec(memory_space=pl.ANY)
IN_SMEM = pl.BlockSpec(memory_space=pltpu.SMEM)


def call(kernel, out_shape, place, *operands, cost=None, scratch=(), last=IN_VMEM, result=IN_VMEM, aliases=None):
    many = isinstance(out_shape, list)
    moved = cost or sum(a.size * a.dtype.itemsize for a in operands)
    return pl.pallas_call(
        kernel,
        out_shape=out_shape,
        in_specs=[IN_SMEM] + [IN_VMEM] * (len(operands) - 1) + [last],
        out_specs=[IN_VMEM] * len(out_shape) if many else result,
        scratch_shapes=scratch,
        input_output_aliases=aliases or {},
        cost_estimate=pl.CostEstimate(flops=moved, bytes_accessed=moved, transcendentals=0),
        compiler_params=pltpu.CompilerParams(vmem_limit_bytes=8 * 2**20),
    )(place, *operands)


def gather_over(block, axis):
    size = lax.axis_size(axis)
    copies = jnp.broadcast_to(block[None], (size,) + block.shape)
    return lax.all_to_all(copies, axis, 0, 0)


def to_lanes(column, position):
    lane = lax.broadcasted_iota(jnp.int32, (column.shape[0], LANES), 1)
    return jnp.sum(jnp.where(position == lane, column, 0.0), axis=0, keepdims=True)


def to_column(lanes, position):
    lane = lax.broadcasted_iota(jnp.int32, (position.shape[0], LANES), 1)
    found = jnp.zeros(lane.shape, lanes.dtype)
    for k in range(lanes.shape[0]):
        found = jnp.where(position == lane + k * LANES, lanes[k : k + 1], found)
    return jnp.sum(found, axis=1, keepdims=True)


def row_iota(rows):
    return lax.broadcasted_iota(jnp.int32, (rows, 1), 0)


def token_position(rows):
    block = rows * C // (ZH * ZL)
    row = row_iota(rows)
    zl, rest = row // (rows // ZL), row % (rows // ZL)
    return rest // block * (ZL * block) + zl * block + rest % block


def target_mask(place_ref, targets_ref, shape):
    column = to_column(targets_ref[...], token_position(shape[0]) + place_ref[1]) - place_ref[2]
    return lax.broadcasted_iota(jnp.int32, shape, 1) == column


def spans(length):
    return [pl.ds(first, min(TILE, length - first)) for first in range(0, length, TILE)]


def logits_kernel(place_ref, rows_ref, head_ref, other_ref, out_ref, kept_ref, sem):
    keep = pltpu.make_async_copy(other_ref, kept_ref, sem)
    keep.start()
    mine = place_ref[0]

    width = head_ref.shape[0]

    def tile(c, part_ref, span):
        rows = rows_ref[:, :, pl.ds(c, 1)].reshape(-1, rows_ref.shape[-1])
        product = lax.dot_general(rows, part_ref[span, :], (((1,), (1,)), ((), ())), preferred_element_type=F32)
        return product.reshape(Y, -1, SUBLANES, span.size)

    for span in spans(width):
        product = tile(mine, head_ref, span)
        for k in range(product.shape[1]):
            out_ref[:, :, pl.ds(k * width + span.start, span.size)] = product[:, k]
    keep.wait()
    for span in spans(width):
        product = tile(C - 1 - mine, kept_ref, span)
        for k in range(product.shape[1]):
            out_ref[:, :, pl.ds(k * width + span.start, span.size)] += product[:, k]


def partial_kernel(place_ref, grad_ref, head_ref, other_ref, spent_ref, out_ref, held_ref, sems):
    mine = place_ref[0]
    _, _, _, rows, slice_width = out_ref.shape
    grad = grad_ref[...].reshape(X * ZL * rows, -1)
    copies = []
    for k, (c, part_ref) in enumerate(((mine, head_ref), (C - 1 - mine, other_ref))):
        for span in spans(slice_width):
            tile = jnp.dot(grad, part_ref[:, span], preferred_element_type=F32).astype(BF16)
            held_ref[k, :, :, :, span] = tile.reshape(X, ZL, rows, span.size)
        copies.append(pltpu.make_async_copy(held_ref.at[k], out_ref.at[:, :, c], sems.at[k]))
        copies[-1].start()
    for copy in copies:
        copy.wait()


def statistics_kernel(place_ref, parts_ref, targets_ref, logits_ref, stats_ref):
    logits = parts_ref[0]
    for y in range(1, Y):
        logits = logits + parts_ref[y]
    width = logits_ref.shape[1]
    logits = jnp.concatenate([logits[:, k : k + width] for k in range(0, logits.shape[1], width)], axis=0)
    logits_ref[...] = logits
    top = jnp.max(logits, axis=1, keepdims=True)
    total = jnp.sum(jnp.exp(logits - top), axis=1, keepdims=True)
    mask = target_mask(place_ref, targets_ref, logits.shape)
    target_logit = jnp.sum(jnp.where(mask, logits, 0.0), axis=1, keepdims=True)
    row = row_iota(logits.shape[0])
    row = to_lanes(top + jnp.log(total), row) + to_lanes(target_logit, row + LANES // 2)
    stats_ref[...] = jnp.broadcast_to(row[None], stats_ref.shape)


def softmax_kernel(place_ref, stats_ref, logits_ref, targets_ref, upstream_ref, loss_ref, grad_ref):
    logits = logits_ref[...]
    rows = logits.shape[0]
    stats = stats_ref[:, 0, :]
    top = jnp.max(stats, axis=0, keepdims=True)
    row = row_iota(rows)
    lse = to_column(top + jnp.log(jnp.sum(jnp.exp(stats - top), axis=0, keepdims=True)), row)
    target_logit = to_column(jnp.sum(stats, axis=0, keepdims=True), row + LANES // 2)
    position = token_position(rows)
    loss_ref[...] = to_lanes(lse - target_logit, position)[:, :rows]
    weight = to_column(upstream_ref[...], position + place_ref[1])
    mask = target_mask(place_ref, targets_ref, logits.shape)
    probability = jnp.exp(logits - lse)
    grad = ((probability - jnp.where(mask, 1.0, 0.0)) * weight).astype(BF16)
    grad_ref[...] = jnp.broadcast_to(grad[None], grad_ref.shape)


def over_x_kernel(place_ref, parts_ref, out_ref):
    blocks, pieces, rows, _ = out_ref.shape
    per_half = blocks // C
    for half in range(C):
        total = 0.0
        for x in range(X):
            for zl in range(ZL):
                total = total + parts_ref[x, zl, half].astype(F32)
        for k in range(per_half * pieces):
            piece = total[k * rows : (k + 1) * rows].astype(BF16)
            out_ref[half * per_half + k // pieces, k % pieces] = piece


def pack_kernel(place_ref, rows_ref, grad_ref, out_ref):
    width, slice_width = grad_ref.shape[-1], rows_ref.shape[-1]
    out_ref[:, :, :width] = grad_ref[...]
    rows = rows_ref[:, :, pl.ds(C - 1 - place_ref[0], 1)]
    out_ref[:, :, out_ref.shape[-1] - slice_width :] = rows.reshape(Y, -1, slice_width)


def pick_kernel(place_ref, rows_ref, out_ref):
    out_ref[...] = rows_ref[:, :, pl.ds(place_ref[0], 1)].reshape(out_ref.shape)


def head_kernel(place_ref, rows_ref, grad_ref, rest_ref, out_ref):
    width, slice_width = out_ref.shape
    rows = rows_ref[...]
    rest_rows = rest_ref[:, :, rest_ref.shape[-1] - slice_width :].reshape(-1, slice_width)

    def dot(grad_ref, span, rows):
        grad = grad_ref[:, :, span].reshape(-1, span.size)
        return lax.dot_general(grad, rows, (((0,), (0,)), ((), ())), preferred_element_type=F32)

    for span in spans(width):
        out_ref[span, :] = (dot(grad_ref, span, rows) + dot(rest_ref, span, rest_rows)).astype(BF16)


def per_device(hidden, head, targets, upstream):
    width, slice_width = head.shape
    token_count = targets.shape[0]
    own = token_count // (Y * C)
    near = (X, ZL, C, own // ZL, slice_width)
    barrier = lax.optimization_barrier

    core = lax.axis_index("core")
    row_first = lax.axis_index(ROW_AXES) * own
    first_column = lax.axis_index(VOCAB_AXES) * width
    hidden, core, row_first, first_column = barrier((hidden, core, row_first, first_column))
    by_z = gather_over(hidden.reshape(-1, 2, slice_width), "zh").reshape(near[2:])

    by_z, head = barrier((by_z, head))
    head_other = lax.ppermute(head, "core", SWAP)
    copies = jnp.broadcast_to(by_z, near).reshape(-1, *near[3:])
    by_x = lax.all_to_all(copies, NEAR_AXES, 0, 0).reshape(near)

    by_x, targets, upstream, core, row_first, first_column = barrier(
        (by_x, targets, upstream, core, row_first, first_column)
    )
    place = jnp.stack([core, row_first, first_column])
    targets, upstream = targets.reshape(-1, LANES), upstream.reshape(-1, LANES)
    out = [jax.ShapeDtypeStruct((Y, SUBLANES, own // SUBLANES * width), F32), jax.ShapeDtypeStruct(head.shape, BF16)]
    sem = [pltpu.SemaphoreType.DMA]
    chip_logits, head_other = call(logits_kernel, out, place, by_x, head, head_other, scratch=sem, last=IN_ANY)
    chip_logits, targets, upstream = barrier((chip_logits, targets, upstream))
    parts = lax.all_to_all(chip_logits, "y", 0, 0)

    out = [jax.ShapeDtypeStruct((own, width), F32), jax.ShapeDtypeStruct((X * ZH * ZL, 1, LANES), F32)]
    logits, stats = call(statistics_kernel, out, place, parts, targets)
    stats = lax.all_to_all(stats, VOCAB_AXES, 0, 0)
    out = [jax.ShapeDtypeStruct((1, own), F32), jax.ShapeDtypeStruct((Y, own, width), BF16)]
    token_loss, grad_rows = call(softmax_kernel, out, place, stats, logits, targets, upstream)

    grad_half = lax.all_to_all(grad_rows, "y", 0, 0)

    held = [pltpu.VMEM((C, X, ZL, *near[3:]), BF16), pltpu.SemaphoreType.DMA((C,))]
    out = jax.ShapeDtypeStruct(near, BF16)
    partial = call(
        partial_kernel, out, place, grad_half, head, head_other, copies.reshape(near),
        scratch=held, last=IN_ANY, result=IN_ANY, aliases={4: 0},
    )
    padded = -(-width // LANES) * LANES
    out = jax.ShapeDtypeStruct((Y, own, padded + slice_width), BF16)
    rest = call(pack_kernel, out, place, by_x, grad_half, cost=PACK_COST)
    rest = lax.ppermute(rest, "core", SWAP)
    over_x = lax.all_to_all(partial.reshape(-1, *near[3:]), NEAR_AXES, 0, 0).reshape(near)
    out = jax.ShapeDtypeStruct((ZH, hidden.shape[0] // 2, 2, slice_width), BF16)
    over_x = call(over_x_kernel, out, place, over_x)
    over_x, by_x, core, grad_half, place = barrier((over_x, by_x, core, grad_half, place))
    over_z = lax.all_to_all(over_x, "zh", 0, 0)

    out = jax.ShapeDtypeStruct((Y * own, slice_width), BF16)
    rows = call(pick_kernel, out, place, by_x, cost=PACK_COST)
    out = jax.ShapeDtypeStruct((width, slice_width), BF16)
    grad_head = call(head_kernel, out, place, rows, grad_half, rest, cost=1)
    over_z, grad_head = barrier((over_z, grad_head))
    grad_hidden = jnp.sum(over_z.astype(F32), axis=0).astype(BF16).reshape(hidden.shape)
    return token_loss[0], grad_hidden, grad_head


def solution(mesh):
    torus = Mesh(mesh.devices.reshape(X, ZH, ZL, Y, C), VOCAB_AXES + ROW_AXES)
    return jax.shard_map(
        per_device,
        mesh=torus,
        in_specs=(P(VOCAB_AXES, ROW_AXES), P(VOCAB_AXES, ROW_AXES), P(), P()),
        out_specs=(P(ROW_AXES), P(VOCAB_AXES, ROW_AXES), P(VOCAB_AXES, ROW_AXES)),
        check_vma=False,
    )
```
